128 devices in a mesh: seq: 32 (over y, z, core), head: 4 (over x).
Axes of the slice: x: 4, y: 4, z: 4, core: 2. Of those that a mesh axis runs over, the one named last changes fastest.
Arguments:
- queries: bfloat16 [32768, 2048], P('seq', 'head'), may hold values from -8 to 8
- key_rows: bfloat16 [32768, 2048], P('seq', 'head'), may hold values from -8 to 8
- value_rows: bfloat16 [32768, 2048], P('seq', 'head'), may hold values from -6 to 6
- grad_out: bfloat16 [32768, 2048], P('seq', 'head'), may hold values from -6 to 6
- cluster_ids: int32 [32768, 16], P('seq', 'head'), may hold values from 0 to 63, as said below
Outputs:
- attended: bfloat16 [32768, 2048], P('seq', 'head')
- grad_query: bfloat16 [32768, 2048], P('seq', 'head')
- grad_key: bfloat16 [32768, 2048], P('seq', 'head')
- grad_value: bfloat16 [32768, 2048], P('seq', 'head')
The draws below stay inside these ranges and needn't reach their ends.
Inputs may be any that keep to these rules, and one draw needn't show every extreme that they name: `cluster_ids`: among the 1024 tokens of one index of seq, at most 24 carry one cluster number in one head's column; in every head some cluster number is carried by exactly 24 tokens of every index of seq.
All inputs are finite; a program needn't handle non-finite values.
Results may differ from the reference program's by a relative error of at most 0.012.
The reference program's roundings to bfloat16 on the way (of `coarse` and `slope`) count: a program that leaves them out, or rounds other values in their place, can miss the bound.
Values may be sent and summed in bfloat16 or wider, within the bound.
No kernel may reach another device: no remote copies, remote signals or barrier semaphores. Data moves between devices by JAX's collectives and lax.ppermute only.
A program may use at most 64 MiB of HBM per device.

```python
import jax
import jax.numpy as jnp
from jax import lax

HEADS = 16
HD = 128
TOK_DEV = 1024
TOKENS = 32768
CLUSTERS = 64
SLOT = 24
N_SEQ = 32


def projected(key):
    result = jnp.clip(jax.random.normal(key, (TOKENS, HEADS, HD), jnp.float32), -6.0, 6.0)
    return result.reshape(TOKENS, HEADS * HD).astype(jnp.bfloat16)


def draw_queries(key, part):
    key = jax.random.fold_in(key, 5)
    return projected(key)


def draw_key_rows(key, part):
    key = jax.random.fold_in(key, 7)
    return projected(key)


def draw_cluster_ids(key, part):
    key = jax.random.fold_in(key, 11)
    blocks = TOKENS // TOK_DEV
    key_heat, key_full, key_noise, key_order = jax.random.split(key, 4)
    spots = CLUSTERS * SLOT
    heat_level = jax.random.randint(key_heat, (HEADS, CLUSTERS), 0, 4)
    saturated = jax.random.randint(key_full, (HEADS,), 0, CLUSTERS)
    jitter = jax.random.randint(key_noise, (blocks, HEADS, CLUSTERS, SLOT), 0, 16)
    penalty = jnp.arange(SLOT, dtype=jnp.int32) * 16 // SLOT
    priority = heat_level[None, :, :, None] * 8 - penalty[None, None, None, :] + jitter
    marked = jnp.arange(CLUSTERS, dtype=jnp.int32)[None, :] == saturated[:, None]
    priority = jnp.where(marked[None, :, :, None], 2000, priority)
    distinct = (priority.reshape(blocks, HEADS, spots) + 64) * spots + jnp.arange(spots, dtype=jnp.int32)
    chosen_spots = lax.top_k(distinct, TOK_DEV)[1]
    chosen_cluster = chosen_spots // SLOT
    shuffle_keys = jax.random.randint(key_order, (blocks, HEADS, TOK_DEV), 0, 2 ** 18) * TOK_DEV + jnp.arange(TOK_DEV, dtype=jnp.int32)
    ordering = jnp.argsort(shuffle_keys, axis=-1)
    assigned = jnp.take_along_axis(chosen_cluster, ordering, axis=-1)
    return assigned.transpose(0, 2, 1).reshape(TOKENS, HEADS).astype(jnp.int32)


def level_of(rng, extent, shards, least, high):
    def one(dim, shards_of):
        draws = jax.random.uniform(jax.random.fold_in(jax.random.fold_in(rng, 6), dim), (shards_of,), jnp.float32, least / len(shards), high / len(shards))
        return jnp.repeat(jnp.exp(draws), extent[dim] // shards_of).reshape((-1,) + (1,) * (len(extent) - dim - 1))

    level = one(*shards[0])
    for cut in shards[1:]:
        level = level * one(*cut)
    return level


def normal_values(stream_key, shape, spread, most, cuts=(), kind=jnp.bfloat16):
    values = jax.random.normal(stream_key, shape, jnp.float32) * spread
    if len(cuts) > 0:
        values = level_of(stream_key, shape, cuts, -0.22, 0.18) * values
    return jnp.clip(values, min=-most, max=most).astype(kind)


def setup_inputs(seed: int = 0) -> dict:
    key_list = jax.random.split(jax.random.key(seed), 6)
    queries = draw_queries(jax.random.fold_in(key_list[5], 71), 0)
    key_rows = draw_key_rows(jax.random.fold_in(key_list[5], 71), 0)
    value_rows = normal_values(key_list[2], (TOKENS, HEADS * HD), 1.0, 6.0, ((0, 32), (1, 4)))
    grad_out = normal_values(key_list[3], (TOKENS, HEADS * HD), 1.0, 6.0, ((0, 32), (1, 4)))
    cluster_ids = draw_cluster_ids(jax.random.fold_in(key_list[5], 71), 0)
    return {"queries": queries, "key_rows": key_rows, "value_rows": value_rows, "grad_out": grad_out, "cluster_ids": cluster_ids}


def probabilities(query_part, key_part, places, factor):
    scores = lax.dot_general(query_part, key_part, (((1,), (1,)), ((), ())), preferred_element_type=jnp.float32) * factor
    allowed = (places[None, :] <= places[:, None]) & (places[None, :] >= 0)
    allowed = allowed | jnp.eye(places.shape[0], dtype=bool)
    scores = jnp.where(allowed, scores, -jnp.inf)
    row_max = jnp.max(scores, axis=1, keepdims=True)
    weights = jnp.exp(scores - row_max)
    return weights / jnp.sum(weights, axis=1, keepdims=True)


def gradients(shares, query_part, key_part, value_part, attended_part, upstream, factor):
    coarse = shares.astype(jnp.bfloat16)
    through = lax.dot_general(upstream, value_part, (((1,), (1,)), ((), ())), preferred_element_type=jnp.float32)
    row_dot = jnp.sum(upstream.astype(jnp.float32) * attended_part.astype(jnp.float32), axis=1, keepdims=True)
    slope = (shares * (through - row_dot)).astype(jnp.bfloat16)
    value_grad = lax.dot_general(coarse, upstream, (((0,), (0,)), ((), ())), preferred_element_type=jnp.float32).astype(jnp.bfloat16)
    query_grad = (factor * jnp.dot(slope, key_part, preferred_element_type=jnp.float32)).astype(jnp.bfloat16)
    key_grad = (factor * lax.dot_general(slope, query_part, (((0,), (0,)), ((), ())), preferred_element_type=jnp.float32)).astype(jnp.bfloat16)
    return query_grad, key_grad, value_grad


def reference(queries, key_rows, value_rows, grad_out, cluster_ids):
    factor = float(HD) ** -0.5
    capacity = N_SEQ * SLOT
    query_all = queries.reshape(TOKENS, HEADS, HD)
    key_all = key_rows.reshape(TOKENS, HEADS, HD)
    value_all = value_rows.reshape(TOKENS, HEADS, HD)
    upstream_all = grad_out.reshape(TOKENS, HEADS, HD)
    gathered = [[], [], [], []]
    for head_num in range(HEADS):
        head_ids = cluster_ids[:, head_num]
        ordering = jnp.argsort(head_ids, stable=True).astype(jnp.int32)
        counts = jnp.sum((head_ids[:, None] == jnp.arange(CLUSTERS, dtype=jnp.int32)[None, :]).astype(jnp.int32), axis=0)
        starts = (jnp.cumsum(counts) - counts).astype(jnp.int32)
        padded = jnp.concatenate([ordering, jnp.zeros((capacity,), jnp.int32)])
        query_head = query_all[:, head_num]
        key_head = key_all[:, head_num]
        value_head = value_all[:, head_num]
        upstream_head = upstream_all[:, head_num]

        def one_cluster(cluster_index):
            members = lax.dynamic_slice(padded, (starts[cluster_index],), (capacity,))
            present = jnp.arange(capacity, dtype=jnp.int32) < counts[cluster_index]
            places = jnp.where(present, members, -1)

            def select_rows(field):
                return jnp.where(present[:, None], field[members], jnp.zeros((), field.dtype))

            query_part = select_rows(query_head)
            key_part = select_rows(key_head)
            value_part = select_rows(value_head)
            upstream = select_rows(upstream_head)
            shares = probabilities(query_part, key_part, places, factor)
            attended_part = jnp.dot(shares.astype(jnp.bfloat16), value_part, preferred_element_type=jnp.float32).astype(jnp.bfloat16)
            query_grad, key_grad, value_grad = gradients(shares, query_part, key_part, value_part, attended_part, upstream, factor)
            return attended_part, query_grad, key_grad, value_grad, jnp.where(present, members, TOKENS)

        results = lax.map(one_cluster, jnp.arange(CLUSTERS, dtype=jnp.int32))
        destination = results[4].reshape(-1)
        for which in range(4):
            placed = jnp.zeros((TOKENS, HD), results[which].dtype).at[destination].set(results[which].reshape(-1, HD), mode="drop")
            gathered[which].append(placed)
    outputs = [jnp.stack(pieces, axis=1).reshape(TOKENS, HEADS * HD) for pieces in gathered]
    return (outputs[0], outputs[1], outputs[2], outputs[3])
```

```python
import functools

import jax
import jax.numpy as jnp
from jax import lax
from jax.experimental import pallas as pl
from jax.experimental.pallas import tpu as pltpu
from jax.sharding import PartitionSpec as P

HEAD = 128
CLUSTERS = 64
SLOT = 24
BLOCK = 256
FIELDS = 4
TIGHT = 148
SORTED_ROUNDS = 2
VMEM = pltpu.CompilerParams(vmem_limit_bytes=60 * 1024 * 1024)
F32 = jnp.float32
BF16 = jnp.bfloat16
I32 = jnp.int32


def iota(shape, dim):
    return lax.broadcasted_iota(I32, shape, dim)


def against(a, b):
    return lax.dot_general(a, b, (((1,), (1,)), ((), ())), preferred_element_type=F32)


def across(a, b):
    return lax.dot_general(a, b, (((0,), (0,)), ((), ())), preferred_element_type=F32)


def smem():
    return pl.BlockSpec(memory_space=pltpu.SMEM)


def whole():
    return pl.BlockSpec(memory_space=pltpu.VMEM)


def pad_rows(capacity):
    return (capacity + SLOT + 7) // 8 * 8


def rank_kernel(ids_ref, pos_ref, count_ref, start_ref):
    heads, tokens = ids_ref.shape
    pairs = heads * CLUSTERS
    marks = jnp.concatenate(
        [
            (ids_ref[h : h + 1, :] == iota((CLUSTERS, tokens), 0)).astype(BF16)
            for h in range(heads)
        ],
        axis=0,
    )
    row, col = iota((pairs, pairs), 0), iota((pairs, pairs), 1)
    earlier = ((col < row) & (col // CLUSTERS == row // CLUSTERS)).astype(BF16)
    count_wide = against(marks, jnp.ones((128, tokens), BF16))
    start_wide = jnp.dot(earlier, count_wide.astype(BF16), preferred_element_type=F32)
    count_line = against(jnp.ones((8, tokens), BF16), marks)
    count_ref[...] = count_line.astype(I32)
    start_ref[...] = against(count_line.astype(BF16), earlier).astype(I32)
    upper = (iota((BLOCK, BLOCK), 0) < iota((BLOCK, BLOCK), 1)).astype(BF16)
    carry = start_wide[:, :1]
    for b in range(tokens // BLOCK):
        part = marks[:, b * BLOCK : (b + 1) * BLOCK]
        before = jnp.dot(part, upper, preferred_element_type=F32) + carry
        wide = part.astype(F32)
        carry = carry + jnp.sum(wide, axis=1, keepdims=True)
        place = wide * before
        for h in range(heads):
            pos_ref[h : h + 1, b * BLOCK : (b + 1) * BLOCK] = jnp.sum(
                place[h * CLUSTERS : (h + 1) * CLUSTERS], axis=0, keepdims=True
            ).astype(I32)


def sort_kernel(pos_ref, q_ref, k_ref, v_ref, g_ref, out_ref):
    tokens = q_ref.shape[0]
    where = pos_ref[pl.ds(pl.program_id(0), 1), :]
    fields = jnp.concatenate([q_ref[...], k_ref[...], v_ref[...], g_ref[...]], axis=1)
    for b in range(tokens // BLOCK):
        select = (where == iota((BLOCK, tokens), 0) + b * BLOCK).astype(BF16)
        rows = jnp.dot(select, fields, preferred_element_type=F32)
        for a in range(FIELDS):
            out_ref[a, b * BLOCK : (b + 1) * BLOCK, :] = rows[:, a * HEAD : (a + 1) * HEAD]


def plan_kernel(count_ref, list_ref, most_ref):
    owners, pairs = count_ref.shape
    rounds = pairs // owners
    counts = count_ref[...].astype(F32)
    row, col = iota((pairs, pairs), 0), iota((pairs, pairs), 1)
    total_line = jnp.sum(counts, axis=0, keepdims=True)
    total_col = jnp.sum(jnp.where(row == col, total_line, 0.0), axis=1, keepdims=True)
    ahead = (total_line > total_col) | ((total_line == total_col) & (col < row))
    rank_col = jnp.sum(ahead.astype(F32), axis=1, keepdims=True)
    at_rank = rank_col == col.astype(F32)
    order_line = jnp.sum(jnp.where(at_rank, row.astype(F32), 0.0), axis=0, keepdims=True)
    size_line = jnp.sum(jnp.where(at_rank, total_col, 0.0), axis=0, keepdims=True)
    device = iota((owners, 1), 0).astype(F32)
    lane = iota((owners, pairs), 1).astype(F32)
    near, far = iota((owners, owners), 0), iota((owners, owners), 1)
    load = jnp.zeros((owners, 1), F32)
    lists = jnp.zeros((owners, 128), F32)
    owned = jnp.zeros((owners, pairs), F32)
    for r in range(rounds):
        if r >= rounds - SORTED_ROUNDS:
            load_line = jnp.sum(jnp.where(near == far, load, 0.0), axis=0, keepdims=True)
            lighter = (load_line < load) | ((load_line == load) & (far < near))
            turn = jnp.sum(lighter.astype(F32), axis=1, keepdims=True)
        elif r % 2 == 0:
            turn = device
        else:
            turn = owners - 1.0 - device
        pick = lane == turn + float(r * owners)
        item = jnp.sum(jnp.where(pick, order_line, 0.0), axis=1, keepdims=True)
        load = load + jnp.sum(jnp.where(pick, size_line, 0.0), axis=1, keepdims=True)
        lists = jnp.where(iota((owners, 128), 1) == r, item, lists)
        owned = jnp.where(lane == item, 1.0, owned)
    list_ref[...] = lists.astype(I32)
    sent = against(counts.astype(BF16), owned.astype(BF16))
    most = jnp.max(jnp.max(sent, axis=1, keepdims=True), axis=0, keepdims=True)
    most_ref[...] = jnp.broadcast_to(most, most_ref.shape).astype(I32)


def pack_kernel(capacity, rounds, list_ref, count_ref, start_ref, sorted_ref, out_ref, table_ref, block):
    d = pl.program_id(0)
    tokens = (sorted_ref.shape[1] - 32) // (count_ref.shape[1] // CLUSTERS)
    padded = block.shape[1]
    offset = 0
    for j in range(rounds):
        item = list_ref[d, j]
        source = item // CLUSTERS * tokens + start_ref[0, item]
        for a in range(FIELDS):
            block[a, pl.ds(offset, SLOT), :] = sorted_ref[a, pl.ds(source, SLOT), :]
        table_ref[item] = d * padded + offset
        offset = offset + count_ref[0, item]
    for a in range(FIELDS):
        out_ref[0, a * capacity : (a + 1) * capacity, :] = block[a, :capacity, :].astype(BF16)


def attend_kernel(
    capacity, rounds, me_ref, list_ref, count_ref, in_ref, out_ref, arrived, leaving, gathered, work, done, used
):
    sources = in_ref.shape[0]
    most = work.shape[1]
    factor = float(HEAD) ** -0.5
    me = me_ref[0]

    def widen(s, _):
        used[s] = 0
        for a in range(FIELDS):
            arrived[s * FIELDS + a, :capacity, :] = in_ref[
                s, a * capacity : (a + 1) * capacity, :
            ].astype(F32)
        return 0

    lax.fori_loop(0, sources, widen, 0)

    def row_block(b):
        rows = slice(b * BLOCK, (b + 1) * BLOCK)
        width = (b + 1) * BLOCK
        query, upstream = work[0, rows, :], work[3, rows, :]
        keys, values = work[1, :width, :], work[2, :width, :]
        scores = against(query, keys) * factor
        allowed = iota((BLOCK, width), 1) <= iota((BLOCK, width), 0) + b * BLOCK
        scores = jnp.where(allowed, scores, -jnp.inf)
        weights = jnp.exp(scores - jnp.max(scores, axis=1, keepdims=True))
        shares = weights * (1.0 / jnp.sum(weights, axis=1, keepdims=True))
        coarse = shares.astype(BF16)
        attended = jnp.dot(coarse, values, preferred_element_type=F32)
        through = against(upstream, values)
        row_dot = jnp.sum(
            upstream.astype(F32) * attended.astype(BF16).astype(F32), axis=1, keepdims=True
        )
        slope = (shares * (through - row_dot)).astype(BF16)
        done[0, rows, :] = attended
        done[1, rows, :] = factor * jnp.dot(slope, keys, preferred_element_type=F32)
        key_grad = factor * across(slope, query)
        value_grad = across(coarse, upstream)
        if b > 0:
            old = slice(0, b * BLOCK)
            done[2, old, :] += key_grad[old]
            done[3, old, :] += value_grad[old]
        done[2, rows, :] = key_grad[rows]
        done[3, rows, :] = value_grad[rows]

    def one(j, _):
        item = list_ref[me, j]

        def collect(s, filled):
            for a in range(FIELDS):
                gathered[a, pl.ds(filled, SLOT), :] = arrived[
                    s * FIELDS + a, pl.ds(used[s], SLOT), :
                ]
            return filled + count_ref[s, item]

        total = lax.fori_loop(0, sources, collect, jnp.int32(0), unroll=4)
        for a in range(FIELDS):
            gathered[a, pl.ds(total, BLOCK), :] = jnp.zeros((BLOCK, HEAD), F32)
        for b in range(most // BLOCK):

            @pl.when(total > b * BLOCK)
            def _():
                rows = slice(b * BLOCK, (b + 1) * BLOCK)
                for a in range(FIELDS):
                    work[a, rows, :] = gathered[a, rows, :].astype(BF16)
                row_block(b)

        def deliver(s, filled):
            place = used[s]
            for a in range(FIELDS):
                leaving[s * FIELDS + a, pl.ds(place, SLOT), :] = done[
                    a, pl.ds(filled, SLOT), :
                ]
            used[s] = place + count_ref[s, item]
            return filled + count_ref[s, item]

        lax.fori_loop(0, sources, deliver, jnp.int32(0), unroll=4)
        return 0

    lax.fori_loop(0, rounds, one, 0)

    def narrow(s, _):
        for a in range(FIELDS):
            out_ref[s, a * capacity : (a + 1) * capacity, :] = leaving[
                s * FIELDS + a, :capacity, :
            ].astype(BF16)
        return 0

    lax.fori_loop(0, sources, narrow, 0)


def unpack_kernel(capacity, table_ref, start_ref, pos_ref, in_ref, o_ref, dq_ref, dk_ref, dv_ref, wide, rows):
    h = pl.program_id(0)
    owners = in_ref.shape[0]
    tokens = o_ref.shape[0]
    padded = pad_rows(capacity)

    @pl.when(h == 0)
    def _():
        def widen(d, _):
            for a in range(FIELDS):
                wide[a, pl.ds(pl.multiple_of(d * padded, 8), capacity), :] = in_ref[
                    d, a * capacity : (a + 1) * capacity, :
                ].astype(F32)
            return 0

        lax.fori_loop(0, owners, widen, 0)

    def put(c, _):
        item = h * CLUSTERS + c
        target = start_ref[0, item]
        source = table_ref[item]
        for a in range(FIELDS):
            rows[a, pl.ds(target, SLOT), :] = wide[a, pl.ds(source, SLOT), :]
        return 0

    lax.fori_loop(0, CLUSTERS, put, 0, unroll=4)
    fields = jnp.concatenate([rows[a, :tokens, :].astype(BF16) for a in range(FIELDS)], axis=1)
    lane = iota((tokens, 128), 1)
    place = jnp.sum(jnp.where(lane == h, pos_ref[...], 0), axis=1, keepdims=True)
    for b in range(tokens // BLOCK):
        part = slice(b * BLOCK, (b + 1) * BLOCK)
        select = (place[part] == iota((BLOCK, tokens), 1)).astype(BF16)
        result = jnp.dot(select, fields, preferred_element_type=F32).astype(BF16)
        for a, ref in enumerate((o_ref, dq_ref, dk_ref, dv_ref)):
            ref[part, :] = result[:, a * HEAD : (a + 1) * HEAD]


def on_device(queries, key_rows, value_rows, grad_out, cluster_ids):
    tokens, heads = cluster_ids.shape
    owners = lax.axis_size("seq")
    pairs = heads * CLUSTERS
    rounds = pairs // owners
    sorted_rows = heads * tokens + 32
    most = owners * SLOT
    me = lax.axis_index("seq").astype(I32).reshape(1)

    place, count, start = pl.pallas_call(
        rank_kernel,
        out_shape=(
            jax.ShapeDtypeStruct((heads, tokens), I32),
            jax.ShapeDtypeStruct((8, pairs), I32),
            jax.ShapeDtypeStruct((8, pairs), I32),
        ),
        in_specs=[whole()],
        out_specs=(whole(),) * 3,
        compiler_params=VMEM,
        name="rank",
    )(cluster_ids.T)

    every_count = lax.all_to_all(
        jnp.broadcast_to(count[:1], (owners, pairs)), "seq", 0, 0, tiled=True
    )

    field_spec = pl.BlockSpec((tokens, HEAD), lambda h: (0, h))
    in_order = pl.pallas_call(
        sort_kernel,
        grid=(heads,),
        out_shape=jax.ShapeDtypeStruct((FIELDS, sorted_rows, HEAD), F32),
        in_specs=[pl.BlockSpec((heads, tokens), lambda h: (0, 0))] + [field_spec] * 4,
        out_specs=pl.BlockSpec((FIELDS, tokens, HEAD), lambda h: (0, h, 0)),
        cost_estimate=pl.CostEstimate(
            flops=2 * heads * tokens * tokens * FIELDS * HEAD,
            bytes_accessed=6 * FIELDS * heads * tokens * HEAD,
            transcendentals=0,
        ),
        compiler_params=VMEM,
        name="sort",
    )(place, queries, key_rows, value_rows, grad_out)

    lists, heaviest = pl.pallas_call(
        plan_kernel,
        out_shape=(
            jax.ShapeDtypeStruct((owners, 128), I32),
            jax.ShapeDtypeStruct((8, 128), I32),
        ),
        in_specs=[whole()],
        out_specs=(whole(),) * 2,
        compiler_params=VMEM,
        name="plan",
    )(every_count)

    token_places = jnp.pad(place.T, ((0, 0), (0, 128 - heads)))

    def exchange(capacity):
        padded = pad_rows(capacity)
        packed = jax.ShapeDtypeStruct((owners, FIELDS * capacity, HEAD), BF16)
        block = pl.BlockSpec((1, FIELDS * capacity, HEAD), lambda d: (d, 0, 0))
        sending, table = pl.pallas_call(
            functools.partial(pack_kernel, capacity, rounds),
            grid=(owners,),
            out_shape=(packed, jax.ShapeDtypeStruct((pairs,), I32)),
            in_specs=[smem(), smem(), smem(), pl.BlockSpec((FIELDS, sorted_rows, HEAD), lambda d: (0, 0, 0))],
            out_specs=(block, smem()),
            scratch_shapes=[pltpu.VMEM((FIELDS, padded, HEAD), F32)],
            compiler_params=VMEM,
            name="pack",
        )(lists, count, start, in_order)
        owned = lax.all_to_all(sending, "seq", 0, 0, tiled=True)
        results = pl.pallas_call(
            functools.partial(attend_kernel, capacity, rounds),
            out_shape=packed,
            in_specs=[smem(), smem(), smem(), whole()],
            out_specs=whole(),
            scratch_shapes=[
                pltpu.VMEM((owners * FIELDS, padded, HEAD), F32),
                pltpu.VMEM((owners * FIELDS, padded, HEAD), F32),
                pltpu.VMEM((FIELDS, most + BLOCK + SLOT, HEAD), F32),
                pltpu.VMEM((FIELDS, most, HEAD), BF16),
                pltpu.VMEM((FIELDS, most + SLOT, HEAD), F32),
                pltpu.SMEM((owners,), I32),
            ],
            compiler_params=VMEM,
            name="attend",
        )(me, lists, every_count, owned)
        returned = lax.all_to_all(results, "seq", 0, 0, tiled=True)
        return pl.pallas_call(
            functools.partial(unpack_kernel, capacity),
            grid=(heads,),
            out_shape=(jax.ShapeDtypeStruct(queries.shape, BF16),) * 4,
            in_specs=[
                smem(),
                smem(),
                pl.BlockSpec((tokens, 128), lambda h: (0, 0)),
                pl.BlockSpec((owners, FIELDS * capacity, HEAD), lambda h: (0, 0, 0)),
            ],
            out_specs=(field_spec,) * 4,
            scratch_shapes=[
                pltpu.VMEM((FIELDS, owners * padded, HEAD), F32),
                pltpu.VMEM((FIELDS, tokens + SLOT, HEAD), F32),
            ],
            compiler_params=VMEM,
            name="unpack",
        )(table, start, token_places, returned)

    return lax.cond(
        heaviest[0, 0] <= TIGHT,
        lambda: exchange(TIGHT),
        lambda: exchange(rounds * SLOT),
    )


def solution(mesh):
    spec = P("seq", "head")
    return jax.shard_map(
        on_device, mesh=mesh, in_specs=(spec,) * 5, out_specs=(spec,) * 4, check_vma=False
    )
```

```python
import functools

import jax
import jax.numpy as jnp
from jax import lax
from jax.experimental import pallas as pl
from jax.experimental.pallas import tpu as pltpu
from jax.sharding import PartitionSpec as P

HEAD = 128
CLUSTERS = 64
SLOT = 24
BLOCK = 256
FIELDS = 4
TIGHT = 144
DEALS = ((0, 0, 0, 0, 0, 0), (27, 20, 16, 8, 9, 1), (2, 0, 5, 26, 20, 29), (11, 30, 23, 3, 17, 6))
OWNERS_AT_ONCE = 8
LOG2_E = 1.4426950408889634
F32 = jnp.float32
BF16 = jnp.bfloat16
I32 = jnp.int32


def iota(shape, dim):
    return lax.broadcasted_iota(I32, shape, dim)


def against(a, b):
    return lax.dot_general(a, b, (((1,), (1,)), ((), ())), preferred_element_type=F32)


def across(a, b):
    return lax.dot_general(a, b, (((0,), (0,)), ((), ())), preferred_element_type=F32)


def limit(mib):
    return pltpu.CompilerParams(vmem_limit_bytes=mib * 1024 * 1024)


def smem():
    return pl.BlockSpec(memory_space=pltpu.SMEM)


def whole():
    return pl.BlockSpec(memory_space=pltpu.VMEM)


def pad_rows(capacity):
    return (capacity + SLOT + 7) // 8 * 8


def rank_kernel(ids_ref, pos_ref, count_ref, start_ref):
    heads, tokens = ids_ref.shape
    pairs = heads * CLUSTERS
    marks = jnp.concatenate(
        [
            (ids_ref[h : h + 1, :] == iota((CLUSTERS, tokens), 0)).astype(BF16)
            for h in range(heads)
        ],
        axis=0,
    )
    row, col = iota((pairs, pairs), 0), iota((pairs, pairs), 1)
    earlier = ((col < row) & (col // CLUSTERS == row // CLUSTERS)).astype(BF16)
    count_wide = against(marks, jnp.ones((128, tokens), BF16))
    start_wide = jnp.dot(earlier, count_wide.astype(BF16), preferred_element_type=F32)
    count_line = against(jnp.ones((count_ref.shape[0], tokens), BF16), marks)
    count_ref[...] = count_line.astype(I32)
    start_ref[...] = against(count_line[:8].astype(BF16), earlier).astype(I32)
    upper = (iota((BLOCK, BLOCK), 0) < iota((BLOCK, BLOCK), 1)).astype(BF16)
    carry = start_wide[:, :1]
    for b in range(tokens // BLOCK):
        part = marks[:, b * BLOCK : (b + 1) * BLOCK]
        before = jnp.dot(part, upper, preferred_element_type=F32) + carry
        wide = part.astype(F32)
        carry = carry + jnp.sum(wide, axis=1, keepdims=True)
        place = wide * before
        for h in range(heads):
            pos_ref[h : h + 1, b * BLOCK : (b + 1) * BLOCK] = jnp.sum(
                place[h * CLUSTERS : (h + 1) * CLUSTERS], axis=0, keepdims=True
            ).astype(I32)


def sort_kernel(pos_ref, q_ref, k_ref, v_ref, g_ref, out_ref):
    tokens = q_ref.shape[0]
    where = pos_ref[pl.ds(pl.program_id(0), 1), :]
    fields = jnp.concatenate([q_ref[...], k_ref[...], v_ref[...], g_ref[...]], axis=1)
    for b in range(tokens // BLOCK):
        select = (where == iota((BLOCK, tokens), 0) + b * BLOCK).astype(BF16)
        rows = jnp.dot(select, fields, preferred_element_type=F32)
        for a in range(FIELDS):
            out_ref[0, a, b * BLOCK : (b + 1) * BLOCK, :] = rows[
                :, a * HEAD : (a + 1) * HEAD
            ].astype(BF16)


def plan_kernel(count_ref, list_ref, most_ref):
    owners, pairs = count_ref.shape
    rounds = pairs // owners
    deals = len(DEALS)
    counts = count_ref[...].astype(F32)
    row, col = iota((pairs, pairs), 0), iota((pairs, pairs), 1)
    total_line = jnp.sum(counts, axis=0, keepdims=True)
    total_col = jnp.sum(jnp.where(row == col, total_line, 0.0), axis=1, keepdims=True)
    ahead = (total_line > total_col) | ((total_line == total_col) & (col < row))
    rank_col = jnp.sum(ahead.astype(F32), axis=1, keepdims=True)
    at_rank = rank_col == col.astype(F32)
    order_line = jnp.sum(jnp.where(at_rank, row.astype(F32), 0.0), axis=0, keepdims=True)
    size_line = jnp.sum(jnp.where(at_rank, total_col, 0.0), axis=0, keepdims=True)
    seats = deals * owners
    seat = iota((seats, 1), 0)
    device, deal = seat % owners, seat // owners
    lane = iota((seats, pairs), 1).astype(F32)
    near, far = iota((seats, seats), 0), iota((seats, seats), 1)
    together = near // owners == far // owners
    load = jnp.zeros((seats, 1), F32)
    lists = jnp.zeros((seats, 128), F32)
    owned = jnp.zeros((seats, pairs), F32)
    for r in range(rounds):
        if r >= len(DEALS[0]):
            load_line = jnp.sum(jnp.where(near == far, load, 0.0), axis=0, keepdims=True)
            lighter = (load_line < load) | ((load_line == load) & (far < near))
            turn = jnp.sum((lighter & together).astype(F32), axis=1, keepdims=True)
        else:
            shift = jnp.zeros((seats, 1), I32)
            for c in range(deals):
                shift = jnp.where(deal == c, DEALS[c][r], shift)
            turn = (device + shift) % owners
            if r % 2 == 1:
                turn = owners - 1 - turn
            turn = turn.astype(F32)
        pick = lane == turn + float(r * owners)
        item = jnp.sum(jnp.where(pick, order_line, 0.0), axis=1, keepdims=True)
        load = load + jnp.sum(jnp.where(pick, size_line, 0.0), axis=1, keepdims=True)
        lists = jnp.where(iota((seats, 128), 1) == r, item, lists)
        owned = jnp.where(lane == item, 1.0, owned)
    sent = against(counts.astype(BF16), owned.astype(BF16))
    heaviest = jnp.max(sent, axis=0, keepdims=True)
    seat_line = iota((1, seats), 1)
    least = None
    for c in range(deals):
        most = jnp.max(
            jnp.where(seat_line // owners == c, heaviest, 0.0), axis=1, keepdims=True
        )
        mine = lists[c * owners : (c + 1) * owners]
        if least is None:
            least, chosen = most, mine
        else:
            chosen = jnp.where(most < least, mine, chosen)
            least = jnp.minimum(least, most)
    list_ref[...] = chosen.astype(I32)
    most_ref[...] = jnp.broadcast_to(least, most_ref.shape).astype(I32)


def pack_kernel(
    capacity, rounds, heads, list_ref, count_ref, start_ref, sorted_ref, out_ref, table_ref, rows, block
):
    step = pl.program_id(0)
    tokens = sorted_ref.shape[2]
    padded = block.shape[2]

    @pl.when(step < heads)
    def _():
        place = pl.multiple_of(step * tokens, 8)
        for a in range(FIELDS):
            rows[a, pl.ds(place, tokens), :] = sorted_ref[0, a].astype(F32)

    @pl.when(step >= heads)
    def _():
        for o in range(OWNERS_AT_ONCE):
            d = (step - heads) * OWNERS_AT_ONCE + o
            items = [list_ref[d, j] for j in range(rounds)]
            counts = [count_ref[0, item] for item in items]
            sources = [item // CLUSTERS * tokens + start_ref[0, item] for item in items]
            offset = 0
            for j in range(rounds):
                for a in range(FIELDS):
                    block[o, a, pl.ds(offset, SLOT), :] = rows[a, pl.ds(sources[j], SLOT), :]
                table_ref[items[j]] = d * padded + offset
                offset = offset + counts[j]
            for a in range(FIELDS):
                out_ref[o, a * capacity : (a + 1) * capacity, :] = block[
                    o, a, :capacity, :
                ].astype(BF16)


def attend_kernel(
    capacity, rounds, me_ref, list_ref, count_ref, in_ref, out_ref, arrived, leaving, gathered, work, done, used
):
    sources = in_ref.shape[0]
    most = work.shape[1]
    factor = float(HEAD) ** -0.5
    me = me_ref[0]

    def widen(s, _):
        used[s] = 0
        for a in range(FIELDS):
            arrived[s * FIELDS + a, :capacity, :] = in_ref[
                s, a * capacity : (a + 1) * capacity, :
            ].astype(F32)
        return 0

    lax.fori_loop(0, sources, widen, 0)

    def cluster(n):
        size = n * BLOCK
        query, keys, values, upstream = (work[a, :size, :] for a in range(FIELDS))
        scale = factor * LOG2_E
        below = iota((BLOCK, BLOCK), 0) <= iota((BLOCK, BLOCK), 1)
        keys_t = gathered[1, :size, :].T.astype(BF16)
        values_t = gathered[2, :size, :].T.astype(BF16)
        up_t = gathered[3, :size, :].T
        cols = [slice(b * BLOCK, (b + 1) * BLOCK) for b in range(n)]
        scores = [against(keys[: (b + 1) * BLOCK], query[cols[b]]) for b in range(n)]
        through = [against(values[: (b + 1) * BLOCK], upstream[cols[b]]) for b in range(n)]
        coarse = []
        slope = []
        for b in range(n):
            s = scores[b]
            last = jnp.where(below, s[b * BLOCK :], -jnp.inf)
            s = last if b == 0 else jnp.concatenate([s[: b * BLOCK], last], axis=0)
            weights = jnp.exp2((s - jnp.max(s, axis=0, keepdims=True)) * scale)
            shares = weights * (1.0 / jnp.sum(weights, axis=0, keepdims=True))
            rough = shares.astype(BF16)
            attended = jnp.dot(values_t[:, : (b + 1) * BLOCK], rough, preferred_element_type=F32)
            done[0, cols[b], :] = attended.T
            row_dot = jnp.sum(up_t[:, cols[b]] * attended.astype(BF16).astype(F32), axis=0, keepdims=True)
            bend = (shares * (through[b] - row_dot)).astype(BF16)
            done[1, cols[b], :] = factor * jnp.dot(keys_t[:, : (b + 1) * BLOCK], bend, preferred_element_type=F32).T
            coarse.append(rough)
            slope.append(bend)
        for k in range(n):
            c = jnp.concatenate([x[cols[k]] for x in coarse[k:]], axis=1)
            done[3, cols[k], :] = jnp.dot(c, upstream[k * BLOCK :], preferred_element_type=F32)
            c = jnp.concatenate([x[cols[k]] for x in slope[k:]], axis=1)
            done[2, cols[k], :] = factor * jnp.dot(c, query[k * BLOCK :], preferred_element_type=F32)

    def one(j, _):
        item = list_ref[me, j]

        def collect(s, filled):
            for a in range(FIELDS):
                gathered[a, pl.ds(filled, SLOT), :] = arrived[
                    s * FIELDS + a, pl.ds(used[s], SLOT), :
                ]
            return filled + count_ref[s, item]

        total = lax.fori_loop(0, sources, collect, jnp.int32(0), unroll=4)
        for a in range(FIELDS):
            gathered[a, pl.ds(total, BLOCK), :] = jnp.zeros((BLOCK, HEAD), F32)
        blocks = most // BLOCK
        for n in range(1, blocks + 1):
            enough = total > (n - 1) * BLOCK
            if n < blocks:
                enough = enough & (total <= n * BLOCK)

            @pl.when(enough)
            def _():
                for a in range(FIELDS):
                    work[a, : n * BLOCK, :] = gathered[a, : n * BLOCK, :].astype(BF16)
                cluster(n)

        def deliver(s, filled):
            place = used[s]
            for a in range(FIELDS):
                leaving[s * FIELDS + a, pl.ds(place, SLOT), :] = done[
                    a, pl.ds(filled, SLOT), :
                ]
            used[s] = place + count_ref[s, item]
            return filled + count_ref[s, item]

        lax.fori_loop(0, sources, deliver, jnp.int32(0), unroll=4)
        return 0

    lax.fori_loop(0, rounds, one, 0)

    def narrow(s, _):
        for a in range(FIELDS):
            out_ref[s, a * capacity : (a + 1) * capacity, :] = leaving[
                s * FIELDS + a, :capacity, :
            ].astype(BF16)
        return 0

    lax.fori_loop(0, sources, narrow, 0)


def unpack_kernel(capacity, table_ref, start_ref, pos_ref, in_ref, o_ref, dq_ref, dk_ref, dv_ref, wide, rows):
    h = pl.program_id(0)
    owners = in_ref.shape[0]
    tokens = o_ref.shape[0]
    padded = pad_rows(capacity)

    @pl.when(h == 0)
    def _():
        def widen(d, _):
            for a in range(FIELDS):
                wide[a, pl.ds(pl.multiple_of(d * padded, 8), capacity), :] = in_ref[
                    d, a * capacity : (a + 1) * capacity, :
                ].astype(F32)
            return 0

        lax.fori_loop(0, owners, widen, 0)

    def put(c, _):
        item = h * CLUSTERS + c
        target = start_ref[0, item]
        source = table_ref[item]
        for a in range(FIELDS):
            rows[a, pl.ds(target, SLOT), :] = wide[a, pl.ds(source, SLOT), :]
        return 0

    lax.fori_loop(0, CLUSTERS, put, 0, unroll=4)
    fields = jnp.concatenate([rows[a, :tokens, :].astype(BF16) for a in range(FIELDS)], axis=1)
    lane = iota((tokens, 128), 1)
    place = jnp.sum(jnp.where(lane == h, pos_ref[...], 0), axis=1, keepdims=True)
    for b in range(tokens // BLOCK):
        part = slice(b * BLOCK, (b + 1) * BLOCK)
        select = (place[part] == iota((BLOCK, tokens), 1)).astype(BF16)
        result = jnp.dot(select, fields, preferred_element_type=F32).astype(BF16)
        for a, ref in enumerate((o_ref, dq_ref, dk_ref, dv_ref)):
            ref[part, :] = result[:, a * HEAD : (a + 1) * HEAD]


def on_device(queries, key_rows, value_rows, grad_out, cluster_ids):
    tokens, heads = cluster_ids.shape
    owners = lax.axis_size("seq")
    pairs = heads * CLUSTERS
    rounds = pairs // owners
    sorted_rows = heads * tokens + SLOT
    most = owners * SLOT
    me = lax.axis_index("seq").astype(I32).reshape(1)

    place, count, start = pl.pallas_call(
        rank_kernel,
        out_shape=(
            jax.ShapeDtypeStruct((heads, tokens), I32),
            jax.ShapeDtypeStruct((owners, pairs), I32),
            jax.ShapeDtypeStruct((8, pairs), I32),
        ),
        in_specs=[whole()],
        out_specs=(whole(),) * 3,
        compiler_params=limit(16),
        name="rank",
    )(cluster_ids.T)

    every_count = lax.all_to_all(count, "seq", 0, 0, tiled=True)

    field_spec = pl.BlockSpec((tokens, HEAD), lambda h: (0, h))
    in_order = pl.pallas_call(
        sort_kernel,
        grid=(heads,),
        out_shape=jax.ShapeDtypeStruct((heads, FIELDS, tokens, HEAD), BF16),
        in_specs=[pl.BlockSpec((heads, tokens), lambda h: (0, 0))] + [field_spec] * 4,
        out_specs=pl.BlockSpec((1, FIELDS, tokens, HEAD), lambda h: (h, 0, 0, 0)),
        cost_estimate=pl.CostEstimate(
            flops=2 * heads * tokens * tokens * FIELDS * HEAD,
            bytes_accessed=4 * FIELDS * heads * tokens * HEAD,
            transcendentals=0,
        ),
        compiler_params=limit(16),
        name="sort",
    )(place, queries, key_rows, value_rows, grad_out)

    lists, heaviest = pl.pallas_call(
        plan_kernel,
        out_shape=(
            jax.ShapeDtypeStruct((owners, 128), I32),
            jax.ShapeDtypeStruct((8, 128), I32),
        ),
        in_specs=[whole()],
        out_specs=(whole(),) * 2,
        compiler_params=limit(16),
        name="plan",
    )(every_count)

    token_places = jnp.pad(place.T, ((0, 0), (0, 128 - heads)))

    def exchange(capacity):
        padded = pad_rows(capacity)
        packed = jax.ShapeDtypeStruct((owners, FIELDS * capacity, HEAD), BF16)
        sending, table = pl.pallas_call(
            functools.partial(pack_kernel, capacity, rounds, heads),
            grid=(heads + owners // OWNERS_AT_ONCE,),
            out_shape=(packed, jax.ShapeDtypeStruct((pairs,), I32)),
            in_specs=[
                smem(),
                smem(),
                smem(),
                pl.BlockSpec(
                    (1, FIELDS, tokens, HEAD), lambda i: (jnp.minimum(i, heads - 1), 0, 0, 0)
                ),
            ],
            out_specs=(
                pl.BlockSpec(
                    (OWNERS_AT_ONCE, FIELDS * capacity, HEAD),
                    lambda i: (jnp.maximum(i - heads, 0), 0, 0),
                ),
                smem(),
            ),
            scratch_shapes=[
                pltpu.VMEM((FIELDS, sorted_rows, HEAD), F32),
                pltpu.VMEM((OWNERS_AT_ONCE, FIELDS, padded, HEAD), F32),
            ],
            compiler_params=limit(24),
            name="pack",
        )(lists, count, start, in_order)
        owned = lax.all_to_all(sending, "seq", 0, 0, tiled=True)
        results = pl.pallas_call(
            functools.partial(attend_kernel, capacity, rounds),
            out_shape=packed,
            in_specs=[smem(), smem(), smem(), whole()],
            out_specs=whole(),
            scratch_shapes=[
                pltpu.VMEM((owners * FIELDS, padded, HEAD), F32),
                pltpu.VMEM((owners * FIELDS, padded, HEAD), F32),
                pltpu.VMEM((FIELDS, most + BLOCK + SLOT, HEAD), F32),
                pltpu.VMEM((FIELDS, most, HEAD), BF16),
                pltpu.VMEM((FIELDS, most + SLOT, HEAD), F32),
                pltpu.SMEM((owners,), I32),
            ],
            compiler_params=limit(48),
            name="attend",
        )(me, lists, every_count, owned)
        returned = lax.all_to_all(results, "seq", 0, 0, tiled=True)
        return pl.pallas_call(
            functools.partial(unpack_kernel, capacity),
            grid=(heads,),
            out_shape=(jax.ShapeDtypeStruct(queries.shape, BF16),) * 4,
            in_specs=[
                smem(),
                smem(),
                pl.BlockSpec((tokens, 128), lambda h: (0, 0)),
                pl.BlockSpec((owners, FIELDS * capacity, HEAD), lambda h: (0, 0, 0)),
            ],
            out_specs=(field_spec,) * 4,
            scratch_shapes=[
                pltpu.VMEM((FIELDS, owners * padded, HEAD), F32),
                pltpu.VMEM((FIELDS, tokens + SLOT, HEAD), F32),
            ],
            compiler_params=limit(36),
            name="unpack",
        )(table, start, token_places, returned)

    return lax.cond(
        heaviest[0, 0] <= TIGHT,
        lambda: exchange(TIGHT),
        lambda: exchange(rounds * SLOT),
    )


def solution(mesh):
    spec = P("seq", "head")
    return jax.shard_map(
        on_device, mesh=mesh, in_specs=(spec,) * 5, out_specs=(spec,) * 4, check_vma=False
    )
```

```python
import functools

import jax
import jax.numpy as jnp
from jax import lax
from jax.experimental import pallas as pl
from jax.experimental.pallas import tpu as pltpu
from jax.sharding import PartitionSpec as P

HEAD = 128
CLUSTERS = 64
SLOT = 24
BLOCK = 256
FIELDS = 4
TIGHT = 144
DEALS = ((0, 0, 0, 0, 0, 0), (27, 20, 16, 8, 9, 1), (2, 0, 5, 26, 20, 29), (11, 30, 23, 3, 17, 6))
CHUNKS = 4
LOG2_E = 1.4426950408889634
F32 = jnp.float32
BF16 = jnp.bfloat16
I32 = jnp.int32


def iota(shape, dim):
    return lax.broadcasted_iota(I32, shape, dim)


def against(a, b):
    return lax.dot_general(a, b, (((1,), (1,)), ((), ())), preferred_element_type=F32)


def across(a, b):
    return lax.dot_general(a, b, (((0,), (0,)), ((), ())), preferred_element_type=F32)


def limit(mib):
    return pltpu.CompilerParams(vmem_limit_bytes=mib * 1024 * 1024)


def smem():
    return pl.BlockSpec(memory_space=pltpu.SMEM)


def whole():
    return pl.BlockSpec(memory_space=pltpu.VMEM)


def outside():
    return pl.BlockSpec(memory_space=pl.ANY)


def pad_rows(capacity):
    return (capacity + SLOT + 7) // 8 * 8


def work_of(flops, moved):
    return pl.CostEstimate(flops=flops, bytes_accessed=moved, transcendentals=0)


def rank_kernel(ids_ref, pos_ref, own_ref, count_ref, start_ref):
    heads, tokens = ids_ref.shape
    pairs = heads * CLUSTERS
    marks = jnp.concatenate(
        [
            (ids_ref[h : h + 1, :] == iota((CLUSTERS, tokens), 0)).astype(BF16)
            for h in range(heads)
        ],
        axis=0,
    )
    row, col = iota((pairs, pairs), 0), iota((pairs, pairs), 1)
    earlier = ((col < row) & (col // CLUSTERS == row // CLUSTERS)).astype(BF16)
    count_wide = against(marks, jnp.ones((128, tokens), BF16))
    start_wide = jnp.dot(earlier, count_wide.astype(BF16), preferred_element_type=F32)
    count_line = against(jnp.ones((8, tokens), BF16), marks)
    own_ref[...] = count_line.astype(I32)
    for k in range(pairs // 128):
        part = count_line[None, :1, k * 128 : (k + 1) * 128].astype(I32)
        count_ref[:, k : k + 1, :] = jnp.broadcast_to(part, (count_ref.shape[0], 1, 128))
    start_ref[...] = against(count_line.astype(BF16), earlier).astype(I32)
    upper = (iota((BLOCK, BLOCK), 0) < iota((BLOCK, BLOCK), 1)).astype(BF16)
    carry = start_wide[:, :1]
    for b in range(tokens // BLOCK):
        part = marks[:, b * BLOCK : (b + 1) * BLOCK]
        before = jnp.dot(part, upper, preferred_element_type=F32) + carry
        wide = part.astype(F32)
        carry = carry + jnp.sum(wide, axis=1, keepdims=True)
        place = wide * before
        for h in range(heads):
            pos_ref[h : h + 1, b * BLOCK : (b + 1) * BLOCK] = jnp.sum(
                place[h * CLUSTERS : (h + 1) * CLUSTERS], axis=0, keepdims=True
            ).astype(I32)


def sort_kernel(pos_ref, q_ref, k_ref, v_ref, g_ref, out_ref, taken, given, in_sems, out_sems):
    heads, tokens = pos_ref.shape
    arriving = []
    for h in range(heads):
        copies = [
            pltpu.make_async_copy(
                ref.at[:, pl.ds(h * HEAD, HEAD)], taken.at[h, a], in_sems.at[h, a]
            )
            for a, ref in enumerate((q_ref, k_ref, v_ref, g_ref))
        ]
        for copy in copies:
            copy.start()
        arriving.append(copies)
    leaving = []
    for h in range(heads):
        for copy in arriving[h]:
            copy.wait()
        fields = jnp.concatenate([taken[h, a] for a in range(FIELDS)], axis=1)
        for b in range(tokens // BLOCK):
            part = slice(b * BLOCK, (b + 1) * BLOCK)
            select = (pos_ref[h : h + 1, :] == iota((BLOCK, tokens), 0) + b * BLOCK).astype(BF16)
            rows = jnp.dot(select, fields, preferred_element_type=F32).astype(BF16)
            for a in range(FIELDS):
                given[h, a, part, :] = rows[:, a * HEAD : (a + 1) * HEAD]
        copy = pltpu.make_async_copy(given.at[h], out_ref.at[h], out_sems.at[h])
        copy.start()
        leaving.append(copy)
    for copy in leaving:
        copy.wait()


def plan_kernel(padded, tokens, me_ref, from_ref, own_ref, start_ref, pack_ref, mine_ref, back_ref, most_ref):
    owners, pairs = from_ref.shape[0], own_ref.shape[1]
    rounds = pairs // owners
    deals = len(DEALS)
    counts = jnp.concatenate(
        [from_ref[:, k : k + 1, :].reshape(owners, 128) for k in range(pairs // 128)], axis=1
    )
    counts = counts.astype(F32)
    row, col = iota((pairs, pairs), 0), iota((pairs, pairs), 1)
    total_line = jnp.sum(counts, axis=0, keepdims=True)
    total_col = jnp.sum(jnp.where(row == col, total_line, 0.0), axis=1, keepdims=True)
    ahead = (total_line > total_col) | ((total_line == total_col) & (col < row))
    rank_col = jnp.sum(ahead.astype(F32), axis=1, keepdims=True)
    at_rank = rank_col == col.astype(F32)
    order_line = jnp.sum(jnp.where(at_rank, row.astype(F32), 0.0), axis=0, keepdims=True)
    size_line = jnp.sum(jnp.where(at_rank, total_col, 0.0), axis=0, keepdims=True)
    seats = deals * owners
    seat = iota((seats, 1), 0)
    device, deal = seat % owners, seat // owners
    lane = iota((seats, pairs), 1).astype(F32)
    near, far = iota((seats, seats), 0), iota((seats, seats), 1)
    together = near // owners == far // owners
    load = jnp.zeros((seats, 1), F32)
    lists = jnp.zeros((seats, 128), F32)
    owned = jnp.zeros((seats, pairs), F32)
    for r in range(rounds):
        if r >= len(DEALS[0]):
            load_line = jnp.sum(jnp.where(near == far, load, 0.0), axis=0, keepdims=True)
            lighter = (load_line < load) | ((load_line == load) & (far < near))
            turn = jnp.sum((lighter & together).astype(F32), axis=1, keepdims=True)
        else:
            shift = jnp.zeros((seats, 1), I32)
            for c in range(deals):
                shift = jnp.where(deal == c, DEALS[c][r], shift)
            turn = (device + shift) % owners
            if r % 2 == 1:
                turn = owners - 1 - turn
            turn = turn.astype(F32)
        pick = lane == turn + float(r * owners)
        item = jnp.sum(jnp.where(pick, order_line, 0.0), axis=1, keepdims=True)
        load = load + jnp.sum(jnp.where(pick, size_line, 0.0), axis=1, keepdims=True)
        lists = jnp.where(iota((seats, 128), 1) == r, item, lists)
        owned = jnp.where(lane == item, 1.0, owned)
    sent = against(counts.astype(BF16), owned.astype(BF16))
    heaviest = jnp.max(sent, axis=0, keepdims=True)
    seat_line = iota((1, seats), 1)
    least = None
    for c in range(deals):
        most = jnp.max(
            jnp.where(seat_line // owners == c, heaviest, 0.0), axis=1, keepdims=True
        )
        mine = lists[c * owners : (c + 1) * owners]
        if least is None:
            least, chosen = most, mine
        else:
            chosen = jnp.where(most < least, mine, chosen)
            least = jnp.minimum(least, most)
    most_ref[0] = jnp.max(least).astype(I32)

    lane = iota((owners, pairs), 1)
    own_line = own_ref[:1, :].astype(F32)
    begin_line = (start_ref[:1, :] + iota((1, pairs), 1) // CLUSTERS * tokens).astype(F32)
    place = jnp.zeros((owners, 1), F32)
    sources, places = jnp.zeros((owners, 128), F32), jnp.zeros((owners, 128), F32)
    back = jnp.zeros((1, pairs), F32)
    home = iota((owners, 1), 0).astype(F32) * float(padded)
    slot = iota((owners, 128), 1)
    for r in range(rounds):
        pick = lane.astype(F32) == chosen[:, r : r + 1]
        sources = jnp.where(
            slot == r, jnp.sum(jnp.where(pick, begin_line, 0.0), axis=1, keepdims=True), sources
        )
        places = jnp.where(slot == r, place, places)
        back = back + jnp.sum(jnp.where(pick, home + place, 0.0), axis=0, keepdims=True)
        place = place + jnp.sum(jnp.where(pick, own_line, 0.0), axis=1, keepdims=True)
    pack_ref[0] = sources.astype(I32)
    pack_ref[1] = places.astype(I32)
    back_ref[...] = jnp.broadcast_to(back, back_ref.shape).astype(I32)

    items = jnp.sum(jnp.where(iota((owners, 128), 0) == me_ref[0], chosen, 0.0), axis=0, keepdims=True)
    square = iota((128, 128), 0), iota((128, 128), 1)
    item_col = jnp.sum(jnp.where(square[0] == square[1], items, 0.0), axis=1, keepdims=True)
    held = (iota((128, pairs), 1).astype(F32) == item_col) & (iota((128, pairs), 0) < rounds)
    mine = against(counts.astype(BF16), held.astype(BF16)).astype(BF16)
    earlier = (square[0] < square[1]).astype(BF16)
    mine_ref[0] = jnp.dot(mine, earlier, preferred_element_type=F32).astype(I32)
    lower = (far < near)[: owners + 8, :owners].astype(BF16)
    filled = jnp.dot(lower, mine, preferred_element_type=F32).astype(I32)
    mine_ref[1] = filled[:owners]
    mine_ref[2] = jnp.broadcast_to(filled[owners : owners + 1], (owners, 128))


def pack_kernel(capacity, rounds, table_ref, sorted_ref, out_ref, taken, rows, block, given, in_sems, out_sems):
    heads, tokens = sorted_ref.shape[0], sorted_ref.shape[2]
    owners = out_ref.shape[0]
    group = owners // CHUNKS
    arriving = [
        pltpu.make_async_copy(sorted_ref.at[h], taken.at[h], in_sems.at[h]) for h in range(heads)
    ]
    for copy in arriving:
        copy.start()
    for h in range(heads):
        arriving[h].wait()
        for a in range(FIELDS):
            rows[a, h * tokens : (h + 1) * tokens, :] = taken[h, a].astype(F32)
    leaving = []
    for g in range(CHUNKS):
        part = pl.ds(g * group, group)

        def one_owner(o, _):
            d = g * group + o
            for j in range(rounds):
                source, target = table_ref[0, d, j], table_ref[1, d, j]
                for a in range(FIELDS):
                    block[a, pl.ds(target, SLOT), :] = rows[a, pl.ds(source, SLOT), :]
            for a in range(FIELDS):
                given[d, a * capacity : (a + 1) * capacity, :] = block[a, :capacity, :].astype(BF16)
            return 0

        lax.fori_loop(0, group, one_owner, 0, unroll=2)
        copy = pltpu.make_async_copy(given.at[part], out_ref.at[part], out_sems.at[g])
        copy.start()
        leaving.append(copy)
    for copy in leaving:
        copy.wait()


def attend_kernel(capacity, rounds, table_ref, in_ref, out_ref, *scratch):
    taken, given, arrived, leaving, gathered, work, done, in_sems, out_sems = scratch
    sources = in_ref.shape[0]
    group = sources // CHUNKS
    most = work.shape[1]
    factor = float(HEAD) ** -0.5
    parts = [pl.ds(g * group, group) for g in range(CHUNKS)]
    arriving = [
        pltpu.make_async_copy(in_ref.at[parts[g]], taken.at[parts[g]], in_sems.at[g])
        for g in range(CHUNKS)
    ]
    for copy in arriving:
        copy.start()

    def widen(s, _):
        for a in range(FIELDS):
            arrived[s * FIELDS + a, :capacity, :] = taken[
                s, a * capacity : (a + 1) * capacity, :
            ].astype(F32)
        return 0

    for g in range(CHUNKS):
        arriving[g].wait()
        lax.fori_loop(g * group, (g + 1) * group, widen, 0, unroll=2)

    def cluster(n):
        size = n * BLOCK
        query, keys, values, upstream = (work[a, :size, :] for a in range(FIELDS))
        scale = factor * LOG2_E
        below = iota((BLOCK, BLOCK), 0) <= iota((BLOCK, BLOCK), 1)
        keys_t = gathered[1, :size, :].T.astype(BF16)
        values_t = gathered[2, :size, :].T.astype(BF16)
        up_t = gathered[3, :size, :].T
        cols = [slice(b * BLOCK, (b + 1) * BLOCK) for b in range(n)]
        upto = [slice(0, (b + 1) * BLOCK) for b in range(n)]
        scores = [against(keys[upto[b]], query[cols[b]]) for b in range(n)]
        through = [against(values[upto[b]], upstream[cols[b]]) for b in range(n)]
        shares = []
        for b in range(n):
            s = scores[b]
            last = jnp.where(below, s[b * BLOCK :], -jnp.inf)
            s = last if b == 0 else jnp.concatenate([s[: b * BLOCK], last], axis=0)
            weights = jnp.exp2((s - jnp.max(s, axis=0, keepdims=True)) * scale)
            shares.append(weights * (1.0 / jnp.sum(weights, axis=0, keepdims=True)))
        coarse = [part.astype(BF16) for part in shares]
        attended = [
            jnp.dot(values_t[:, upto[b]], coarse[b], preferred_element_type=F32) for b in range(n)
        ]
        for b in range(n):
            done[0, cols[b], :] = attended[b].T
        for k in range(n):
            part = jnp.concatenate([coarse[b][cols[k]] for b in range(k, n)], axis=1)
            done[3, cols[k], :] = jnp.dot(part, upstream[k * BLOCK :], preferred_element_type=F32)
        slope = []
        for b in range(n):
            row_dot = jnp.sum(
                up_t[:, cols[b]] * attended[b].astype(BF16).astype(F32), axis=0, keepdims=True
            )
            slope.append((shares[b] * (through[b] - row_dot)).astype(BF16))
        for b in range(n):
            done[1, cols[b], :] = (
                factor * jnp.dot(keys_t[:, upto[b]], slope[b], preferred_element_type=F32).T
            )
        for k in range(n):
            part = jnp.concatenate([slope[b][cols[k]] for b in range(k, n)], axis=1)
            done[2, cols[k], :] = factor * jnp.dot(
                part, query[k * BLOCK :], preferred_element_type=F32
            )

    def one(j, _):
        for s in range(sources):
            place, filled = table_ref[0, s, j], table_ref[1, s, j]
            for a in range(FIELDS):
                gathered[a, pl.ds(filled, SLOT), :] = arrived[
                    s * FIELDS + a, pl.ds(place, SLOT), :
                ]
        total = table_ref[2, 0, j]
        for a in range(FIELDS):
            gathered[a, pl.ds(total, BLOCK), :] = jnp.zeros((BLOCK, HEAD), F32)
        blocks = most // BLOCK
        for n in range(1, blocks + 1):
            enough = total > (n - 1) * BLOCK
            if n < blocks:
                enough = enough & (total <= n * BLOCK)

            @pl.when(enough)
            def _():
                for a in range(FIELDS):
                    work[a, : n * BLOCK, :] = gathered[a, : n * BLOCK, :].astype(BF16)
                cluster(n)

        for s in range(sources):
            place, filled = table_ref[0, s, j], table_ref[1, s, j]
            for a in range(FIELDS):
                leaving[s * FIELDS + a, pl.ds(place, SLOT), :] = done[a, pl.ds(filled, SLOT), :]
        return 0

    lax.fori_loop(0, rounds, one, 0)

    def narrow(s, _):
        for a in range(FIELDS):
            given[s, a * capacity : (a + 1) * capacity, :] = leaving[
                s * FIELDS + a, :capacity, :
            ].astype(BF16)
        return 0

    going = []
    for g in range(CHUNKS):
        lax.fori_loop(g * group, (g + 1) * group, narrow, 0, unroll=2)
        copy = pltpu.make_async_copy(given.at[parts[g]], out_ref.at[parts[g]], out_sems.at[g])
        copy.start()
        going.append(copy)
    for copy in going:
        copy.wait()


def unpack_kernel(capacity, back_ref, start_ref, pos_ref, in_ref, *refs):
    out_refs, (taken, wide, rows, given, in_sems, out_sems) = refs[:FIELDS], refs[FIELDS:]
    owners, heads, tokens = in_ref.shape[0], given.shape[0], given.shape[2]
    padded = wide.shape[1] // owners
    group = owners // CHUNKS
    parts = [pl.ds(g * group, group) for g in range(CHUNKS)]
    arriving = [
        pltpu.make_async_copy(in_ref.at[parts[g]], taken.at[parts[g]], in_sems.at[g])
        for g in range(CHUNKS)
    ]
    for copy in arriving:
        copy.start()

    def widen(d, _):
        place = pl.multiple_of(d * padded, 8)
        for a in range(FIELDS):
            wide[a, pl.ds(place, capacity), :] = taken[
                d, a * capacity : (a + 1) * capacity, :
            ].astype(F32)
        return 0

    for g in range(CHUNKS):
        arriving[g].wait()
        lax.fori_loop(g * group, (g + 1) * group, widen, 0, unroll=2)
    leaving = []
    for h in range(heads):
        for c in range(CLUSTERS):
            target = start_ref[0, h * CLUSTERS + c]
            source = back_ref[0, h * CLUSTERS + c]
            for a in range(FIELDS):
                rows[a, pl.ds(target, SLOT), :] = wide[a, pl.ds(source, SLOT), :]
        fields = jnp.concatenate([rows[a, :tokens, :].astype(BF16) for a in range(FIELDS)], axis=1)
        for b in range(tokens // BLOCK):
            part = slice(b * BLOCK, (b + 1) * BLOCK)
            select = (pos_ref[part, h : h + 1] == iota((BLOCK, tokens), 1)).astype(BF16)
            result = jnp.dot(select, fields, preferred_element_type=F32).astype(BF16)
            for a in range(FIELDS):
                given[h, a, part, :] = result[:, a * HEAD : (a + 1) * HEAD]
        for a, ref in enumerate(out_refs):
            copy = pltpu.make_async_copy(
                given.at[h, a], ref.at[:, pl.ds(h * HEAD, HEAD)], out_sems.at[h, a]
            )
            copy.start()
            leaving.append(copy)
    for copy in leaving:
        copy.wait()


def on_device(queries, key_rows, value_rows, grad_out, cluster_ids):
    tokens, heads = cluster_ids.shape
    owners = lax.axis_size("seq")
    pairs = heads * CLUSTERS
    rounds = pairs // owners
    sorted_rows = heads * tokens + SLOT
    most = owners * SLOT
    me = lax.axis_index("seq").astype(I32).reshape(1)

    place, count, to_all, start = pl.pallas_call(
        rank_kernel,
        out_shape=(
            jax.ShapeDtypeStruct((heads, tokens), I32),
            jax.ShapeDtypeStruct((8, pairs), I32),
            jax.ShapeDtypeStruct((owners, 8, 128), I32),
            jax.ShapeDtypeStruct((8, pairs), I32),
        ),
        in_specs=[whole()],
        out_specs=(whole(),) * 4,
        compiler_params=limit(16),
        name="rank",
    )(cluster_ids.T)
    token_places = jnp.pad(place.T, ((0, 0), (0, 128 - heads)))

    from_all = lax.all_to_all(to_all, "seq", 0, 0, tiled=True)

    all_fields = pltpu.VMEM((heads, FIELDS, tokens, HEAD), BF16)
    in_order = pl.pallas_call(
        sort_kernel,
        out_shape=jax.ShapeDtypeStruct((heads, FIELDS, tokens, HEAD), BF16),
        in_specs=[whole()] + [outside()] * 4,
        out_specs=outside(),
        scratch_shapes=[
            all_fields,
            all_fields,
            pltpu.SemaphoreType.DMA((heads, FIELDS)),
            pltpu.SemaphoreType.DMA((heads,)),
        ],
        cost_estimate=work_of(
            2 * heads * tokens * tokens * FIELDS * HEAD, 4 * FIELDS * heads * tokens * HEAD
        ),
        compiler_params=limit(60),
        name="sort",
    )(place, queries, key_rows, value_rows, grad_out)

    padded = pad_rows(rounds * SLOT)
    pack_table, mine_table, back_table, heaviest = pl.pallas_call(
        functools.partial(plan_kernel, padded, tokens),
        out_shape=(
            jax.ShapeDtypeStruct((2, owners, 128), I32),
            jax.ShapeDtypeStruct((3, owners, 128), I32),
            jax.ShapeDtypeStruct((8, pairs), I32),
            jax.ShapeDtypeStruct((1,), I32),
        ),
        in_specs=[smem()] + [whole()] * 3,
        out_specs=(whole(), whole(), whole(), smem()),
        compiler_params=limit(16),
        name="plan",
    )(me, from_all, count, start)

    def exchange(capacity):
        block = (owners, FIELDS * capacity, HEAD)
        packed = jax.ShapeDtypeStruct(block, BF16)
        chunk_sems = pltpu.SemaphoreType.DMA((CHUNKS,))
        sending = pl.pallas_call(
            functools.partial(pack_kernel, capacity, rounds),
            out_shape=packed,
            in_specs=[smem(), outside()],
            out_specs=outside(),
            scratch_shapes=[
                all_fields,
                pltpu.VMEM((FIELDS, heads * tokens + SLOT, HEAD), F32),
                pltpu.VMEM((FIELDS, pad_rows(capacity), HEAD), F32),
                pltpu.VMEM(block, BF16),
                pltpu.SemaphoreType.DMA((heads,)),
                chunk_sems,
            ],
            compiler_params=limit(60),
            name="pack",
        )(pack_table, in_order)
        owned = lax.all_to_all(sending, "seq", 0, 0, tiled=True)
        results = pl.pallas_call(
            functools.partial(attend_kernel, capacity, rounds),
            out_shape=packed,
            in_specs=[smem(), outside()],
            out_specs=outside(),
            scratch_shapes=[
                pltpu.VMEM(block, BF16),
                pltpu.VMEM(block, BF16),
                pltpu.VMEM((owners * FIELDS, pad_rows(capacity), HEAD), F32),
                pltpu.VMEM((owners * FIELDS, pad_rows(capacity), HEAD), F32),
                pltpu.VMEM((FIELDS, most + BLOCK + SLOT, HEAD), F32),
                pltpu.VMEM((FIELDS, most, HEAD), BF16),
                pltpu.VMEM((FIELDS, most + SLOT, HEAD), F32),
                chunk_sems,
                chunk_sems,
            ],
            compiler_params=limit(60),
            name="attend",
        )(mine_table, owned)
        returned = lax.all_to_all(results, "seq", 0, 0, tiled=True)
        return pl.pallas_call(
            functools.partial(unpack_kernel, capacity),
            out_shape=(jax.ShapeDtypeStruct(queries.shape, BF16),) * 4,
            in_specs=[smem(), smem(), whole(), outside()],
            out_specs=(outside(),) * 4,
            scratch_shapes=[
                pltpu.VMEM(block, BF16),
                pltpu.VMEM((FIELDS, owners * padded, HEAD), F32),
                pltpu.VMEM((FIELDS, tokens + SLOT, HEAD), F32),
                all_fields,
                chunk_sems,
                pltpu.SemaphoreType.DMA((heads, FIELDS)),
            ],
            compiler_params=limit(60),
            name="unpack",
        )(back_table, start, token_places, returned)

    return lax.cond(
        heaviest[0] <= TIGHT,
        lambda: exchange(TIGHT),
        lambda: exchange(rounds * SLOT),
    )


def solution(mesh):
    spec = P("seq", "head")
    return jax.shard_map(
        on_device, mesh=mesh, in_specs=(spec,) * 5, out_specs=(spec,) * 4, check_vma=False
    )
```

```python
import functools

import jax
import jax.numpy as jnp
from jax import lax
from jax.experimental import pallas as pl
from jax.experimental.pallas import tpu as pltpu
from jax.sharding import PartitionSpec as P

HEAD = 128
CLUSTERS = 64
SLOT = 24
BLOCK = 256
FIELDS = 4
TIGHT = 144
DEALS = ((0, 0, 0, 0, 0, 0), (27, 20, 16, 8, 9, 1), (2, 0, 5, 26, 20, 29), (11, 30, 23, 3, 17, 6))
LOG2_E = 1.4426950408889634
F32 = jnp.float32
BF16 = jnp.bfloat16
I32 = jnp.int32


def iota(shape, dim):
    return lax.broadcasted_iota(I32, shape, dim)


def against(a, b):
    return lax.dot_general(a, b, (((1,), (1,)), ((), ())), preferred_element_type=F32)


def across(a, b):
    return lax.dot_general(a, b, (((0,), (0,)), ((), ())), preferred_element_type=F32)


def limit(mib):
    return pltpu.CompilerParams(vmem_limit_bytes=mib * 1024 * 1024)


def smem():
    return pl.BlockSpec(memory_space=pltpu.SMEM)


def whole():
    return pl.BlockSpec(memory_space=pltpu.VMEM)


def outside():
    return pl.BlockSpec(memory_space=pl.ANY)


def pad_rows(capacity):
    return (capacity + SLOT + 7) // 8 * 8


def work_of(flops, moved):
    return pl.CostEstimate(flops=flops, bytes_accessed=moved, transcendentals=0)


def rank_kernel(ids_ref, pos_ref, column_ref, own_ref, count_ref, start_ref):
    heads, tokens = ids_ref.shape
    pairs = heads * CLUSTERS
    marks = jnp.concatenate(
        [
            (ids_ref[h : h + 1, :] == iota((CLUSTERS, tokens), 0)).astype(BF16)
            for h in range(heads)
        ],
        axis=0,
    )
    row, col = iota((pairs, pairs), 0), iota((pairs, pairs), 1)
    earlier = ((col < row) & (col // CLUSTERS == row // CLUSTERS)).astype(BF16)
    count_wide = against(marks, jnp.ones((128, tokens), BF16))
    start_wide = jnp.dot(earlier, count_wide.astype(BF16), preferred_element_type=F32)
    count_line = against(jnp.ones((8, tokens), BF16), marks)
    own_ref[...] = count_line.astype(I32)
    for k in range(pairs // 128):
        part = count_line[None, :1, k * 128 : (k + 1) * 128].astype(I32)
        count_ref[:, k : k + 1, :] = jnp.broadcast_to(part, (count_ref.shape[0], 1, 128))
    start_ref[...] = against(count_line.astype(BF16), earlier).astype(I32)
    upper = (iota((BLOCK, BLOCK), 0) < iota((BLOCK, BLOCK), 1)).astype(BF16)
    carry = start_wide[:, :1]
    for b in range(tokens // BLOCK):
        part = marks[:, b * BLOCK : (b + 1) * BLOCK]
        before = jnp.dot(part, upper, preferred_element_type=F32) + carry
        wide = part.astype(F32)
        carry = carry + jnp.sum(wide, axis=1, keepdims=True)
        place = wide * before
        lines = jnp.concatenate(
            [
                jnp.sum(place[h * CLUSTERS : (h + 1) * CLUSTERS], axis=0, keepdims=True)
                for h in range(heads)
            ]
            + [jnp.zeros((128 - heads, BLOCK), F32)],
            axis=0,
        )
        part = slice(b * BLOCK, (b + 1) * BLOCK)
        pos_ref[:, part] = lines[:heads].astype(I32)
        column_ref[part, :] = lines.T.astype(I32)


def sort_kernel(pos_ref, q_ref, k_ref, v_ref, g_ref, out_ref, taken, given, in_sems, out_sems):
    heads, tokens = pos_ref.shape
    arriving = []
    for h in range(heads):
        copies = [
            pltpu.make_async_copy(
                ref.at[:, pl.ds(h * HEAD, HEAD)], taken.at[h, a], in_sems.at[h, a]
            )
            for a, ref in enumerate((q_ref, k_ref, v_ref, g_ref))
        ]
        for copy in copies:
            copy.start()
        arriving.append(copies)
    leaving = []
    for h in range(heads):
        for copy in arriving[h]:
            copy.wait()
        fields = jnp.concatenate([taken[h, a] for a in range(FIELDS)], axis=1)
        for b in range(tokens // BLOCK):
            part = slice(b * BLOCK, (b + 1) * BLOCK)
            select = (pos_ref[h : h + 1, :] == iota((BLOCK, tokens), 0) + b * BLOCK).astype(BF16)
            rows = jnp.dot(select, fields, preferred_element_type=F32).astype(BF16)
            for a in range(FIELDS):
                given[h, a, part, :] = rows[:, a * HEAD : (a + 1) * HEAD]
        copy = pltpu.make_async_copy(given.at[h], out_ref.at[h], out_sems.at[h])
        copy.start()
        leaving.append(copy)
    for copy in leaving:
        copy.wait()


def plan_kernel(padded, tokens, me_ref, from_ref, own_ref, start_ref, pack_ref, mine_ref, back_ref, most_ref):
    owners, pairs = from_ref.shape[0], own_ref.shape[1]
    rounds = pairs // owners
    deals = len(DEALS)
    counts = jnp.concatenate(
        [from_ref[:, k : k + 1, :].reshape(owners, 128) for k in range(pairs // 128)], axis=1
    )
    counts = counts.astype(F32)
    row, col = iota((pairs, pairs), 0), iota((pairs, pairs), 1)
    total_line = jnp.sum(counts, axis=0, keepdims=True)
    total_col = jnp.sum(jnp.where(row == col, total_line, 0.0), axis=1, keepdims=True)
    ahead = (total_line > total_col) | ((total_line == total_col) & (col < row))
    rank_col = jnp.sum(ahead.astype(F32), axis=1, keepdims=True)
    at_rank = rank_col == col.astype(F32)
    order_line = jnp.sum(jnp.where(at_rank, row.astype(F32), 0.0), axis=0, keepdims=True)
    size_line = jnp.sum(jnp.where(at_rank, total_col, 0.0), axis=0, keepdims=True)
    seats = deals * owners
    seat = iota((seats, 1), 0)
    device, deal = seat % owners, seat // owners
    lane = iota((seats, pairs), 1).astype(F32)
    near, far = iota((seats, seats), 0), iota((seats, seats), 1)
    together = near // owners == far // owners
    load = jnp.zeros((seats, 1), F32)
    lists = jnp.zeros((seats, 128), F32)
    owned = jnp.zeros((seats, pairs), F32)
    for r in range(rounds):
        if r >= len(DEALS[0]):
            load_line = jnp.sum(jnp.where(near == far, load, 0.0), axis=0, keepdims=True)
            lighter = (load_line < load) | ((load_line == load) & (far < near))
            turn = jnp.sum((lighter & together).astype(F32), axis=1, keepdims=True)
        else:
            shift = jnp.zeros((seats, 1), I32)
            for c in range(deals):
                shift = jnp.where(deal == c, DEALS[c][r], shift)
            turn = (device + shift) % owners
            if r % 2 == 1:
                turn = owners - 1 - turn
            turn = turn.astype(F32)
        pick = lane == turn + float(r * owners)
        item = jnp.sum(jnp.where(pick, order_line, 0.0), axis=1, keepdims=True)
        load = load + jnp.sum(jnp.where(pick, size_line, 0.0), axis=1, keepdims=True)
        lists = jnp.where(iota((seats, 128), 1) == r, item, lists)
        owned = jnp.where(lane == item, 1.0, owned)
    sent = against(counts.astype(BF16), owned.astype(BF16))
    heaviest = jnp.max(sent, axis=0, keepdims=True)
    seat_line = iota((1, seats), 1)
    least = None
    for c in range(deals):
        most = jnp.max(
            jnp.where(seat_line // owners == c, heaviest, 0.0), axis=1, keepdims=True
        )
        mine = lists[c * owners : (c + 1) * owners]
        if least is None:
            least, chosen = most, mine
        else:
            chosen = jnp.where(most < least, mine, chosen)
            least = jnp.minimum(least, most)
    most_ref[0] = jnp.max(least).astype(I32)

    lane = iota((owners, pairs), 1)
    own_line = own_ref[:1, :].astype(F32)
    begin_line = (start_ref[:1, :] + iota((1, pairs), 1) // CLUSTERS * tokens).astype(F32)
    place = jnp.zeros((owners, 1), F32)
    sources, places = jnp.zeros((owners, 128), F32), jnp.zeros((owners, 128), F32)
    back = jnp.zeros((1, pairs), F32)
    home = iota((owners, 1), 0).astype(F32) * float(padded)
    slot = iota((owners, 128), 1)
    for r in range(rounds):
        pick = lane.astype(F32) == chosen[:, r : r + 1]
        sources = jnp.where(
            slot == r, jnp.sum(jnp.where(pick, begin_line, 0.0), axis=1, keepdims=True), sources
        )
        places = jnp.where(slot == r, place, places)
        back = back + jnp.sum(jnp.where(pick, home + place, 0.0), axis=0, keepdims=True)
        place = place + jnp.sum(jnp.where(pick, own_line, 0.0), axis=1, keepdims=True)
    pack_ref[0] = sources.astype(I32)
    pack_ref[1] = places.astype(I32)
    back_ref[...] = jnp.broadcast_to(back, back_ref.shape).astype(I32)

    items = jnp.sum(jnp.where(iota((owners, 128), 0) == me_ref[0], chosen, 0.0), axis=0, keepdims=True)
    square = iota((128, 128), 0), iota((128, 128), 1)
    item_col = jnp.sum(jnp.where(square[0] == square[1], items, 0.0), axis=1, keepdims=True)
    held = (iota((128, pairs), 1).astype(F32) == item_col) & (iota((128, pairs), 0) < rounds)
    mine = against(counts.astype(BF16), held.astype(BF16)).astype(BF16)
    earlier = (square[0] < square[1]).astype(BF16)
    mine_ref[0] = jnp.dot(mine, earlier, preferred_element_type=F32).astype(I32)
    lower = (far < near)[: owners + 8, :owners].astype(BF16)
    filled = jnp.dot(lower, mine, preferred_element_type=F32).astype(I32)
    mine_ref[1] = filled[:owners]
    mine_ref[2] = jnp.broadcast_to(filled[owners : owners + 1], (owners, 128))


def pack_kernel(capacity, rounds, table_ref, sorted_ref, out_ref, taken, rows, block, in_sems):
    heads, tokens = sorted_ref.shape[0], sorted_ref.shape[2]
    owners = out_ref.shape[0]
    arriving = [
        pltpu.make_async_copy(sorted_ref.at[h], taken.at[h], in_sems.at[h]) for h in range(heads)
    ]
    for copy in arriving:
        copy.start()
    for h in range(heads):
        arriving[h].wait()
        for a in range(FIELDS):
            rows[a, h * tokens : (h + 1) * tokens, :] = taken[h, a].astype(F32)

    def one_owner(d, _):
        for j in range(rounds):
            source, target = table_ref[0, d, j], table_ref[1, d, j]
            for a in range(FIELDS):
                block[a, pl.ds(target, SLOT), :] = rows[a, pl.ds(source, SLOT), :]
        for a in range(FIELDS):
            out_ref[d, a * capacity : (a + 1) * capacity, :] = block[a, :capacity, :].astype(BF16)
        return 0

    lax.fori_loop(0, owners, one_owner, 0, unroll=2)


def attend_kernel(capacity, rounds, table_ref, in_ref, out_ref, *scratch):
    arrived, leaving, gathered, work, done = scratch
    sources = in_ref.shape[0]
    most = work.shape[1]
    factor = float(HEAD) ** -0.5

    def widen(s, _):
        for a in range(FIELDS):
            arrived[s * FIELDS + a, :capacity, :] = in_ref[
                s, a * capacity : (a + 1) * capacity, :
            ].astype(F32)
        return 0

    lax.fori_loop(0, sources, widen, 0, unroll=2)

    def cluster(n):
        size = n * BLOCK
        query, keys, values, upstream = (work[a, :size, :] for a in range(FIELDS))
        scale = factor * LOG2_E
        below = iota((BLOCK, BLOCK), 0) <= iota((BLOCK, BLOCK), 1)
        keys_t = gathered[1, :size, :].T.astype(BF16)
        values_t = gathered[2, :size, :].T.astype(BF16)
        up_t = gathered[3, :size, :].T
        cols = [slice(b * BLOCK, (b + 1) * BLOCK) for b in range(n)]
        upto = [slice(0, (b + 1) * BLOCK) for b in range(n)]
        scores = [against(keys[upto[b]], query[cols[b]]) for b in range(n)]
        through = [against(values[upto[b]], upstream[cols[b]]) for b in range(n)]
        shares = []
        for b in range(n):
            s = scores[b]
            last = jnp.where(below, s[b * BLOCK :], -jnp.inf)
            s = last if b == 0 else jnp.concatenate([s[: b * BLOCK], last], axis=0)
            weights = jnp.exp2((s - jnp.max(s, axis=0, keepdims=True)) * scale)
            shares.append(weights * (1.0 / jnp.sum(weights, axis=0, keepdims=True)))
        coarse = [part.astype(BF16) for part in shares]
        attended = [
            jnp.dot(values_t[:, upto[b]], coarse[b], preferred_element_type=F32) for b in range(n)
        ]
        for b in range(n):
            done[0, cols[b], :] = attended[b].T
        for k in range(n):
            part = jnp.concatenate([coarse[b][cols[k]] for b in range(k, n)], axis=1)
            done[3, cols[k], :] = jnp.dot(part, upstream[k * BLOCK :], preferred_element_type=F32)
        slope = []
        for b in range(n):
            row_dot = jnp.sum(
                up_t[:, cols[b]] * attended[b].astype(BF16).astype(F32), axis=0, keepdims=True
            )
            slope.append((shares[b] * (through[b] - row_dot)).astype(BF16))
        for b in range(n):
            done[1, cols[b], :] = (
                factor * jnp.dot(keys_t[:, upto[b]], slope[b], preferred_element_type=F32).T
            )
        for k in range(n):
            part = jnp.concatenate([slope[b][cols[k]] for b in range(k, n)], axis=1)
            done[2, cols[k], :] = factor * jnp.dot(
                part, query[k * BLOCK :], preferred_element_type=F32
            )

    def one(j, _):
        for s in range(sources):
            place, filled = table_ref[0, s, j], table_ref[1, s, j]
            for a in range(FIELDS):
                gathered[a, pl.ds(filled, SLOT), :] = arrived[
                    s * FIELDS + a, pl.ds(place, SLOT), :
                ]
        total = table_ref[2, 0, j]
        for a in range(FIELDS):
            gathered[a, pl.ds(total, BLOCK), :] = jnp.zeros((BLOCK, HEAD), F32)
        blocks = most // BLOCK
        for n in range(1, blocks + 1):
            enough = total > (n - 1) * BLOCK
            if n < blocks:
                enough = enough & (total <= n * BLOCK)

            @pl.when(enough)
            def _():
                for a in range(FIELDS):
                    work[a, : n * BLOCK, :] = gathered[a, : n * BLOCK, :].astype(BF16)
                cluster(n)

        for s in range(sources):
            place, filled = table_ref[0, s, j], table_ref[1, s, j]
            for a in range(FIELDS):
                leaving[s * FIELDS + a, pl.ds(place, SLOT), :] = done[a, pl.ds(filled, SLOT), :]
        return 0

    lax.fori_loop(0, rounds, one, 0)

    def narrow(s, _):
        for a in range(FIELDS):
            out_ref[s, a * capacity : (a + 1) * capacity, :] = leaving[
                s * FIELDS + a, :capacity, :
            ].astype(BF16)
        return 0

    lax.fori_loop(0, sources, narrow, 0, unroll=2)


def unpack_kernel(capacity, back_ref, start_ref, pos_ref, in_ref, *refs):
    out_refs, (wide, rows, given, out_sems) = refs[:FIELDS], refs[FIELDS:]
    owners, heads, tokens = in_ref.shape[0], given.shape[0], given.shape[2]
    padded = wide.shape[1] // owners

    def widen(d, _):
        place = pl.multiple_of(d * padded, 8)
        for a in range(FIELDS):
            wide[a, pl.ds(place, capacity), :] = in_ref[
                d, a * capacity : (a + 1) * capacity, :
            ].astype(F32)
        return 0

    lax.fori_loop(0, owners, widen, 0, unroll=2)
    leaving = []
    for h in range(heads):
        for c in range(CLUSTERS):
            target = start_ref[0, h * CLUSTERS + c]
            source = back_ref[0, h * CLUSTERS + c]
            for a in range(FIELDS):
                rows[a, pl.ds(target, SLOT), :] = wide[a, pl.ds(source, SLOT), :]
        fields = jnp.concatenate([rows[a, :tokens, :].astype(BF16) for a in range(FIELDS)], axis=1)
        for b in range(tokens // BLOCK):
            part = slice(b * BLOCK, (b + 1) * BLOCK)
            select = (pos_ref[part, h : h + 1] == iota((BLOCK, tokens), 1)).astype(BF16)
            result = jnp.dot(select, fields, preferred_element_type=F32).astype(BF16)
            for a in range(FIELDS):
                given[h, a, part, :] = result[:, a * HEAD : (a + 1) * HEAD]
        for a, ref in enumerate(out_refs):
            copy = pltpu.make_async_copy(
                given.at[h, a], ref.at[:, pl.ds(h * HEAD, HEAD)], out_sems.at[h, a]
            )
            copy.start()
            leaving.append(copy)
    for copy in leaving:
        copy.wait()


def on_device(queries, key_rows, value_rows, grad_out, cluster_ids):
    tokens, heads = cluster_ids.shape
    owners = lax.axis_size("seq")
    pairs = heads * CLUSTERS
    rounds = pairs // owners
    sorted_rows = heads * tokens + SLOT
    most = owners * SLOT
    me = lax.axis_index("seq").astype(I32).reshape(1)

    place, token_places, count, to_all, start = pl.pallas_call(
        rank_kernel,
        out_shape=(
            jax.ShapeDtypeStruct((heads, tokens), I32),
            jax.ShapeDtypeStruct((tokens, 128), I32),
            jax.ShapeDtypeStruct((8, pairs), I32),
            jax.ShapeDtypeStruct((owners, 8, 128), I32),
            jax.ShapeDtypeStruct((8, pairs), I32),
        ),
        in_specs=[whole()],
        out_specs=(whole(),) * 5,
        compiler_params=limit(16),
        name="rank",
    )(cluster_ids.T)

    from_all = lax.all_to_all(to_all, "seq", 0, 0, tiled=True)

    all_fields = pltpu.VMEM((heads, FIELDS, tokens, HEAD), BF16)
    in_order = pl.pallas_call(
        sort_kernel,
        out_shape=jax.ShapeDtypeStruct((heads, FIELDS, tokens, HEAD), BF16),
        in_specs=[whole()] + [outside()] * 4,
        out_specs=outside(),
        scratch_shapes=[
            all_fields,
            all_fields,
            pltpu.SemaphoreType.DMA((heads, FIELDS)),
            pltpu.SemaphoreType.DMA((heads,)),
        ],
        cost_estimate=work_of(
            2 * heads * tokens * tokens * FIELDS * HEAD, 4 * FIELDS * heads * tokens * HEAD
        ),
        compiler_params=limit(59),
        name="sort",
    )(place, queries, key_rows, value_rows, grad_out)

    padded = pad_rows(rounds * SLOT)
    pack_table, mine_table, back_table, heaviest = pl.pallas_call(
        functools.partial(plan_kernel, padded, tokens),
        out_shape=(
            jax.ShapeDtypeStruct((2, owners, 128), I32),
            jax.ShapeDtypeStruct((3, owners, 128), I32),
            jax.ShapeDtypeStruct((8, pairs), I32),
            jax.ShapeDtypeStruct((1,), I32),
        ),
        in_specs=[smem()] + [whole()] * 3,
        out_specs=(whole(), whole(), whole(), smem()),
        compiler_params=limit(16),
        name="plan",
    )(me, from_all, count, start)

    def exchange(capacity):
        block = (owners, FIELDS * capacity, HEAD)
        packed = jax.ShapeDtypeStruct(block, BF16)
        sending = pl.pallas_call(
            functools.partial(pack_kernel, capacity, rounds),
            out_shape=packed,
            in_specs=[smem(), outside()],
            out_specs=whole(),
            scratch_shapes=[
                all_fields,
                pltpu.VMEM((FIELDS, heads * tokens + SLOT, HEAD), F32),
                pltpu.VMEM((FIELDS, pad_rows(capacity), HEAD), F32),
                pltpu.SemaphoreType.DMA((heads,)),
            ],
            compiler_params=limit(24),
            name="pack",
        )(pack_table, in_order)
        owned = lax.all_to_all(sending, "seq", 0, 0, tiled=True)
        results = pl.pallas_call(
            functools.partial(attend_kernel, capacity, rounds),
            out_shape=packed,
            in_specs=[smem(), whole()],
            out_specs=whole(),
            scratch_shapes=[
                pltpu.VMEM((owners * FIELDS, pad_rows(capacity), HEAD), F32),
                pltpu.VMEM((owners * FIELDS, pad_rows(capacity), HEAD), F32),
                pltpu.VMEM((FIELDS, most + BLOCK + SLOT, HEAD), F32),
                pltpu.VMEM((FIELDS, most, HEAD), BF16),
                pltpu.VMEM((FIELDS, most + SLOT, HEAD), F32),
            ],
            compiler_params=limit(36 if capacity <= TIGHT else 44),
            name="attend",
        )(mine_table, owned)
        returned = lax.all_to_all(results, "seq", 0, 0, tiled=True)
        return pl.pallas_call(
            functools.partial(unpack_kernel, capacity),
            out_shape=(jax.ShapeDtypeStruct(queries.shape, BF16),) * 4,
            in_specs=[smem(), smem(), whole(), whole()],
            out_specs=(outside(),) * 4,
            scratch_shapes=[
                pltpu.VMEM((FIELDS, owners * padded, HEAD), F32),
                pltpu.VMEM((FIELDS, tokens + SLOT, HEAD), F32),
                all_fields,
                pltpu.SemaphoreType.DMA((heads, FIELDS)),
            ],
            compiler_params=limit(28),
            name="unpack",
        )(back_table, start, token_places, returned)

    return lax.cond(
        heaviest[0] <= TIGHT,
        lambda: exchange(TIGHT),
        lambda: exchange(rounds * SLOT),
    )


def solution(mesh):
    spec = P("seq", "head")
    return jax.shard_map(
        on_device, mesh=mesh, in_specs=(spec,) * 5, out_specs=(spec,) * 4, check_vma=False
    )
```

```python
import functools

import jax
import jax.numpy as jnp
from jax import lax
from jax.experimental import pallas as pl
from jax.experimental.pallas import tpu as pltpu
from jax.sharding import PartitionSpec as P

HEAD = 128
CLUSTERS = 64
SLOT = 24
BLOCK = 256
FIELDS = 4
TIGHT = 144
DEALS = ((0, 0, 0, 0, 0, 0), (27, 20, 16, 8, 9, 1), (2, 0, 5, 26, 20, 29), (11, 30, 23, 3, 17, 6))
LOG2_E = 1.4426950408889634
F32 = jnp.float32
BF16 = jnp.bfloat16
I32 = jnp.int32


def iota(shape, dim):
    return lax.broadcasted_iota(I32, shape, dim)


def against(a, b):
    return lax.dot_general(a, b, (((1,), (1,)), ((), ())), preferred_element_type=F32)


def across(a, b):
    return lax.dot_general(a, b, (((0,), (0,)), ((), ())), preferred_element_type=F32)


def limit(mib):
    return pltpu.CompilerParams(vmem_limit_bytes=mib * 1024 * 1024)


def smem():
    return pl.BlockSpec(memory_space=pltpu.SMEM)


def whole():
    return pl.BlockSpec(memory_space=pltpu.VMEM)


def in_hbm():
    return pl.BlockSpec(memory_space=pltpu.HBM)


def pad_rows(capacity):
    return (capacity + SLOT + 7) // 8 * 8


def work_of(flops, moved):
    return pl.CostEstimate(flops=flops, bytes_accessed=moved, transcendentals=0)


def marks_of(ids_ref):
    heads, tokens = ids_ref.shape
    return jnp.concatenate(
        [
            (ids_ref[h : h + 1, :] == iota((CLUSTERS, tokens), 0)).astype(BF16)
            for h in range(heads)
        ],
        axis=0,
    )


def count_kernel(ids_ref, count_ref):
    count_line = against(jnp.ones((8, ids_ref.shape[1]), BF16), marks_of(ids_ref))
    for k in range(count_line.shape[1] // 128):
        part = count_line[None, :1, k * 128 : (k + 1) * 128].astype(I32)
        count_ref[:, k : k + 1, :] = jnp.broadcast_to(part, (count_ref.shape[0], 1, 128))


def sort_kernel(ids_ref, q_ref, k_ref, v_ref, g_ref, out_ref, place_ref, own_ref, start_ref, *scratch):
    taken, given, in_sems, out_sems = scratch
    heads, tokens = ids_ref.shape
    pairs = heads * CLUSTERS
    arriving = []
    for h in range(heads):
        copies = [
            pltpu.make_async_copy(
                ref.at[:, pl.ds(h * HEAD, HEAD)], taken.at[h, a], in_sems.at[h, a]
            )
            for a, ref in enumerate((q_ref, k_ref, v_ref, g_ref))
        ]
        for copy in copies:
            copy.start()
        arriving.append(copies)

    marks = marks_of(ids_ref)
    row, col = iota((pairs, pairs), 0), iota((pairs, pairs), 1)
    earlier = ((col < row) & (col // CLUSTERS == row // CLUSTERS)).astype(BF16)
    count_wide = against(marks, jnp.ones((128, tokens), BF16))
    start_wide = jnp.dot(earlier, count_wide.astype(BF16), preferred_element_type=F32)
    count_line = against(jnp.ones((8, tokens), BF16), marks)
    own_ref[...] = count_line.astype(I32)
    start_ref[...] = against(count_line.astype(BF16), earlier).astype(I32)
    upper = (iota((BLOCK, BLOCK), 0) < iota((BLOCK, BLOCK), 1)).astype(BF16)
    carry = start_wide[:, :1]
    for b in range(tokens // BLOCK):
        part = marks[:, b * BLOCK : (b + 1) * BLOCK]
        before = jnp.dot(part, upper, preferred_element_type=F32) + carry
        wide = part.astype(F32)
        carry = carry + jnp.sum(wide, axis=1, keepdims=True)
        place = wide * before
        for h in range(heads):
            place_ref[h : h + 1, b * BLOCK : (b + 1) * BLOCK] = jnp.sum(
                place[h * CLUSTERS : (h + 1) * CLUSTERS], axis=0, keepdims=True
            ).astype(I32)

    leaving = []
    for h in range(heads):
        for copy in arriving[h]:
            copy.wait()
        fields = jnp.concatenate([taken[h, a] for a in range(FIELDS)], axis=1)
        for b in range(tokens // BLOCK):
            part = slice(b * BLOCK, (b + 1) * BLOCK)
            select = (place_ref[h : h + 1, :] == iota((BLOCK, tokens), 0) + b * BLOCK).astype(BF16)
            rows = jnp.dot(select, fields, preferred_element_type=F32).astype(BF16)
            for a in range(FIELDS):
                given[h, a, part, :] = rows[:, a * HEAD : (a + 1) * HEAD]
            part = pl.ds(b * BLOCK, BLOCK)
            copy = pltpu.make_async_copy(
                given.at[h, :, part], out_ref.at[h, :, part], out_sems.at[h, b]
            )
            copy.start()
            leaving.append(copy)
    for copy in leaving:
        copy.wait()


def plan(padded, tokens, me_ref, from_ref, own_ref, start_ref, pack_ref, mine_ref, back_ref, most_ref):
    owners, pairs = from_ref.shape[0], own_ref.shape[1]
    rounds = pairs // owners
    deals = len(DEALS)
    counts = jnp.concatenate(
        [from_ref[:, k : k + 1, :].reshape(owners, 128) for k in range(pairs // 128)], axis=1
    )
    counts = counts.astype(F32)
    row, col = iota((pairs, pairs), 0), iota((pairs, pairs), 1)
    total_line = jnp.sum(counts, axis=0, keepdims=True)
    total_col = jnp.sum(jnp.where(row == col, total_line, 0.0), axis=1, keepdims=True)
    ahead = (total_line > total_col) | ((total_line == total_col) & (col < row))
    rank_col = jnp.sum(ahead.astype(F32), axis=1, keepdims=True)
    at_rank = rank_col == col.astype(F32)
    order_line = jnp.sum(jnp.where(at_rank, row.astype(F32), 0.0), axis=0, keepdims=True)
    size_line = jnp.sum(jnp.where(at_rank, total_col, 0.0), axis=0, keepdims=True)
    seats = deals * owners
    seat = iota((seats, 1), 0)
    device, deal = seat % owners, seat // owners
    lane = iota((seats, pairs), 1).astype(F32)
    near, far = iota((seats, seats), 0), iota((seats, seats), 1)
    together = near // owners == far // owners
    load = jnp.zeros((seats, 1), F32)
    lists = jnp.zeros((seats, 128), F32)
    owned = jnp.zeros((seats, pairs), F32)
    for r in range(rounds):
        if r >= len(DEALS[0]):
            load_line = jnp.sum(jnp.where(near == far, load, 0.0), axis=0, keepdims=True)
            lighter = (load_line < load) | ((load_line == load) & (far < near))
            turn = jnp.sum((lighter & together).astype(F32), axis=1, keepdims=True)
        else:
            shift = jnp.zeros((seats, 1), I32)
            for c in range(deals):
                shift = jnp.where(deal == c, DEALS[c][r], shift)
            turn = (device + shift) % owners
            if r % 2 == 1:
                turn = owners - 1 - turn
            turn = turn.astype(F32)
        pick = lane == turn + float(r * owners)
        item = jnp.sum(jnp.where(pick, order_line, 0.0), axis=1, keepdims=True)
        load = load + jnp.sum(jnp.where(pick, size_line, 0.0), axis=1, keepdims=True)
        lists = jnp.where(iota((seats, 128), 1) == r, item, lists)
        owned = jnp.where(lane == item, 1.0, owned)
    sent = against(counts.astype(BF16), owned.astype(BF16))
    heaviest = jnp.max(sent, axis=0, keepdims=True)
    seat_line = iota((1, seats), 1)
    least = None
    for c in range(deals):
        most = jnp.max(
            jnp.where(seat_line // owners == c, heaviest, 0.0), axis=1, keepdims=True
        )
        mine = lists[c * owners : (c + 1) * owners]
        if least is None:
            least, chosen = most, mine
        else:
            chosen = jnp.where(most < least, mine, chosen)
            least = jnp.minimum(least, most)
    most_ref[0] = jnp.max(least).astype(I32)

    lane = iota((owners, pairs), 1)
    own_line = own_ref[:1, :].astype(F32)
    begin_line = (start_ref[:1, :] + iota((1, pairs), 1) // CLUSTERS * tokens).astype(F32)
    place = jnp.zeros((owners, 1), F32)
    sources, places = jnp.zeros((owners, 128), F32), jnp.zeros((owners, 128), F32)
    back = jnp.zeros((1, pairs), F32)
    home = iota((owners, 1), 0).astype(F32) * float(padded)
    slot = iota((owners, 128), 1)
    for r in range(rounds):
        pick = lane.astype(F32) == chosen[:, r : r + 1]
        sources = jnp.where(
            slot == r, jnp.sum(jnp.where(pick, begin_line, 0.0), axis=1, keepdims=True), sources
        )
        places = jnp.where(slot == r, place, places)
        back = back + jnp.sum(jnp.where(pick, home + place, 0.0), axis=0, keepdims=True)
        place = place + jnp.sum(jnp.where(pick, own_line, 0.0), axis=1, keepdims=True)
    pack_ref[0] = sources.astype(I32)
    pack_ref[1] = places.astype(I32)
    back_ref[...] = jnp.broadcast_to(back, back_ref.shape).astype(I32)

    items = jnp.sum(jnp.where(iota((owners, 128), 0) == me_ref[0], chosen, 0.0), axis=0, keepdims=True)
    square = iota((128, 128), 0), iota((128, 128), 1)
    item_col = jnp.sum(jnp.where(square[0] == square[1], items, 0.0), axis=1, keepdims=True)
    held = (iota((128, pairs), 1).astype(F32) == item_col) & (iota((128, pairs), 0) < rounds)
    mine = against(counts.astype(BF16), held.astype(BF16)).astype(BF16)
    earlier = (square[0] < square[1]).astype(BF16)
    mine_ref[0] = jnp.dot(mine, earlier, preferred_element_type=F32).astype(I32)
    lower = (far < near)[: owners + 8, :owners].astype(BF16)
    filled = jnp.dot(lower, mine, preferred_element_type=F32).astype(I32)
    mine_ref[1] = filled[:owners]
    mine_ref[2] = jnp.broadcast_to(filled[owners : owners + 1], (owners, 128))


def fill(capacity, rounds, table, rows, block, out_ref):
    def one_owner(d, _):
        for j in range(rounds):
            source = table[0, d, j]
            target = jnp.minimum(table[1, d, j], capacity)
            for a in range(FIELDS):
                block[a, pl.ds(target, SLOT), :] = rows[a, pl.ds(source, SLOT), :]
        for a in range(FIELDS):
            out_ref[d, a * capacity : (a + 1) * capacity, :] = block[a, :capacity, :].astype(BF16)
        return 0

    lax.fori_loop(0, out_ref.shape[0], one_owner, 0, unroll=2)


def widen_heads(sorted_ref, rows):
    heads, _, tokens, _ = sorted_ref.shape
    for h in range(heads):
        for a in range(FIELDS):
            rows[a, h * tokens : (h + 1) * tokens, :] = sorted_ref[h, a].astype(F32)


def pack_kernel(capacity, rounds, table_ref, sorted_ref, out_ref, rows, block):
    widen_heads(sorted_ref, rows)
    fill(capacity, rounds, table_ref, rows, block, out_ref)


def plan_and_pack_kernel(capacity, rounds, padded, me_ref, from_ref, own_ref, start_ref, sorted_ref, *refs):
    out_ref, pack_ref, mine_ref, back_ref, most_ref, taken, rows, block, table, in_sems, table_sem = refs
    heads, _, tokens, _ = sorted_ref.shape
    arriving = [
        pltpu.make_async_copy(sorted_ref.at[h], taken.at[h], in_sems.at[h]) for h in range(heads)
    ]
    for copy in arriving:
        copy.start()
    plan(padded, tokens, me_ref, from_ref, own_ref, start_ref, pack_ref, mine_ref, back_ref, most_ref)
    copy = pltpu.make_async_copy(pack_ref, table, table_sem)
    copy.start()
    for h in range(heads):
        arriving[h].wait()
        for a in range(FIELDS):
            rows[a, h * tokens : (h + 1) * tokens, :] = taken[h, a].astype(F32)
    copy.wait()
    fill(capacity, rounds, table, rows, block, out_ref)


def attend_kernel(capacity, rounds, table_ref, in_ref, out_ref, *scratch):
    arrived, leaving, gathered, work, done = scratch
    sources = in_ref.shape[0]
    most = work.shape[1]
    factor = float(HEAD) ** -0.5

    def widen(s, _):
        for a in range(FIELDS):
            arrived[s * FIELDS + a, :capacity, :] = in_ref[
                s, a * capacity : (a + 1) * capacity, :
            ].astype(F32)
        return 0

    lax.fori_loop(0, sources, widen, 0, unroll=2)

    def cluster(n):
        size = n * BLOCK
        query, keys, values = (work[a, :size, :] for a in range(FIELDS - 1))
        scale = factor * LOG2_E
        below = iota((BLOCK, BLOCK), 0) <= iota((BLOCK, BLOCK), 1)
        keys_t = gathered[1, :size, :].T.astype(BF16)
        values_t = gathered[2, :size, :].T.astype(BF16)
        up_t = gathered[3, :size, :].T
        upstream_t = up_t.astype(BF16)
        cols = [slice(b * BLOCK, (b + 1) * BLOCK) for b in range(n)]
        upto = [slice(0, (b + 1) * BLOCK) for b in range(n)]
        scores = [against(keys[upto[b]], query[cols[b]]) for b in range(n)]
        weights, inverse = [], []
        for b in range(n):
            s = scores[b]
            last = jnp.where(below, s[b * BLOCK :], -jnp.inf)
            s = last if b == 0 else jnp.concatenate([s[: b * BLOCK], last], axis=0)
            weights.append(jnp.exp2((s - jnp.max(s, axis=0, keepdims=True)) * scale))
            inverse.append(1.0 / jnp.sum(weights[b], axis=0, keepdims=True))
        coarse = [(weights[b] * inverse[b]).astype(BF16) for b in range(n)]
        attended = [
            jnp.dot(values_t[:, upto[b]], coarse[b], preferred_element_type=F32)
            for b in range(n)
        ]
        for b in range(n):
            done[0, cols[b], :] = attended[b].T
        through = [
            jnp.dot(values[upto[b]], upstream_t[:, cols[b]], preferred_element_type=F32)
            for b in range(n)
        ]
        for k in range(n):
            part = jnp.concatenate([coarse[b][cols[k]] for b in range(k, n)], axis=1)
            done[3, cols[k], :] = against(part, upstream_t[:, k * BLOCK :])
        slope = []
        for b in range(n):
            row_dot = jnp.sum(
                up_t[:, cols[b]] * attended[b].astype(BF16).astype(F32), axis=0, keepdims=True
            )
            slope.append((weights[b] * ((through[b] - row_dot) * inverse[b])).astype(BF16))
        for b in range(n):
            done[1, cols[b], :] = (
                factor * jnp.dot(keys_t[:, upto[b]], slope[b], preferred_element_type=F32).T
            )
        for k in range(n):
            part = jnp.concatenate([slope[b][cols[k]] for b in range(k, n)], axis=1)
            done[2, cols[k], :] = factor * jnp.dot(
                part, query[k * BLOCK :], preferred_element_type=F32
            )

    def one(j, _):
        for s in range(sources):
            place, filled = jnp.minimum(table_ref[0, s, j], capacity), table_ref[1, s, j]
            for a in range(FIELDS):
                gathered[a, pl.ds(filled, SLOT), :] = arrived[
                    s * FIELDS + a, pl.ds(place, SLOT), :
                ]
        total = table_ref[2, 0, j]
        for a in range(FIELDS):
            gathered[a, pl.ds(total, BLOCK), :] = jnp.zeros((BLOCK, HEAD), F32)
        blocks = most // BLOCK
        for n in range(1, blocks + 1):
            enough = total > (n - 1) * BLOCK
            if n < blocks:
                enough = enough & (total <= n * BLOCK)

            @pl.when(enough)
            def _():
                for a in range(FIELDS - 1):
                    work[a, : n * BLOCK, :] = gathered[a, : n * BLOCK, :].astype(BF16)
                cluster(n)

        for s in range(sources):
            place, filled = jnp.minimum(table_ref[0, s, j], capacity), table_ref[1, s, j]
            for a in range(FIELDS):
                leaving[s * FIELDS + a, pl.ds(place, SLOT), :] = done[a, pl.ds(filled, SLOT), :]
        return 0

    lax.fori_loop(0, rounds, one, 0)

    def narrow(s, _):
        for a in range(FIELDS):
            out_ref[s, a * capacity : (a + 1) * capacity, :] = leaving[
                s * FIELDS + a, :capacity, :
            ].astype(BF16)
        return 0

    lax.fori_loop(0, sources, narrow, 0, unroll=2)


def unpack_kernel(capacity, back_ref, start_ref, place_ref, in_ref, *refs):
    out_refs, (wide, rows, given, out_sems) = refs[:FIELDS], refs[FIELDS:]
    owners, heads, tokens = in_ref.shape[0], given.shape[0], given.shape[2]
    padded = wide.shape[1] // owners

    def widen(d, _):
        place = pl.multiple_of(d * padded, 8)
        for a in range(FIELDS):
            wide[a, pl.ds(place, capacity), :] = in_ref[
                d, a * capacity : (a + 1) * capacity, :
            ].astype(F32)
        return 0

    lax.fori_loop(0, owners, widen, 0, unroll=2)
    lines = jnp.concatenate(
        [place_ref[...].astype(F32), jnp.zeros((128 - heads, tokens), F32)], axis=0
    )
    columns = lines.T.astype(I32)
    leaving = []
    for h in range(heads):
        for c in range(CLUSTERS):
            target = start_ref[0, h * CLUSTERS + c]
            source = back_ref[0, h * CLUSTERS + c]
            for a in range(FIELDS):
                rows[a, pl.ds(target, SLOT), :] = wide[a, pl.ds(source, SLOT), :]
        fields = jnp.concatenate([rows[a, :tokens, :].astype(BF16) for a in range(FIELDS)], axis=1)
        for b in range(tokens // BLOCK):
            part = slice(b * BLOCK, (b + 1) * BLOCK)
            select = (columns[part, h : h + 1] == iota((BLOCK, tokens), 1)).astype(BF16)
            result = jnp.dot(select, fields, preferred_element_type=F32).astype(BF16)
            for a in range(FIELDS):
                given[h, a, part, :] = result[:, a * HEAD : (a + 1) * HEAD]
            for a, ref in enumerate(out_refs):
                copy = pltpu.make_async_copy(
                    given.at[h, a, pl.ds(b * BLOCK, BLOCK)],
                    ref.at[pl.ds(b * BLOCK, BLOCK), pl.ds(h * HEAD, HEAD)],
                    out_sems.at[h, a, b],
                )
                copy.start()
                leaving.append(copy)
    for copy in leaving:
        copy.wait()


def on_device(queries, key_rows, value_rows, grad_out, cluster_ids):
    tokens, heads = cluster_ids.shape
    owners = lax.axis_size("seq")
    pairs = heads * CLUSTERS
    rounds = pairs // owners
    most = owners * SLOT
    me = lax.axis_index("seq").astype(I32).reshape(1)

    ids = cluster_ids.T
    padded = pad_rows(rounds * SLOT)
    blocks = tokens // BLOCK
    dma = pltpu.SemaphoreType.DMA
    all_fields = pltpu.VMEM((heads, FIELDS, tokens, HEAD), BF16)
    all_rows = pltpu.VMEM((FIELDS, heads * tokens + SLOT, HEAD), F32)

    to_all = pl.pallas_call(
        count_kernel,
        out_shape=jax.ShapeDtypeStruct((owners, 8, 128), I32),
        in_specs=[whole()],
        out_specs=whole(),
        compiler_params=limit(16),
        name="count",
    )(ids)
    from_all = lax.all_to_all(to_all, "seq", 0, 0, tiled=True)

    in_order, place, count, start = pl.pallas_call(
        sort_kernel,
        out_shape=(
            jax.ShapeDtypeStruct((heads, FIELDS, tokens, HEAD), BF16),
            jax.ShapeDtypeStruct((heads, tokens), I32),
            jax.ShapeDtypeStruct((8, pairs), I32),
            jax.ShapeDtypeStruct((8, pairs), I32),
        ),
        in_specs=[whole()] + [in_hbm()] * 4,
        out_specs=(in_hbm(),) + (whole(),) * 3,
        scratch_shapes=[
            all_fields,
            all_fields,
            dma((heads, FIELDS)),
            dma((heads, blocks)),
        ],
        cost_estimate=work_of(
            2 * heads * tokens * tokens * FIELDS * HEAD, 4 * FIELDS * heads * tokens * HEAD
        ),
        compiler_params=limit(24),
        name="sort",
    )(
        ids,
        *(
            pltpu.with_memory_space_constraint(field, pltpu.HBM)
            for field in (queries, key_rows, value_rows, grad_out)
        ),
    )

    sending, pack_table, mine_table, back_table, heaviest = pl.pallas_call(
        functools.partial(plan_and_pack_kernel, TIGHT, rounds, padded),
        out_shape=(
            jax.ShapeDtypeStruct((owners, FIELDS * TIGHT, HEAD), BF16),
            jax.ShapeDtypeStruct((2, owners, 128), I32),
            jax.ShapeDtypeStruct((3, owners, 128), I32),
            jax.ShapeDtypeStruct((8, pairs), I32),
            jax.ShapeDtypeStruct((1,), I32),
        ),
        in_specs=[smem()] + [whole()] * 3 + [in_hbm()],
        out_specs=(whole(),) * 4 + (smem(),),
        scratch_shapes=[
            all_fields,
            all_rows,
            pltpu.VMEM((FIELDS, pad_rows(TIGHT), HEAD), F32),
            pltpu.SMEM((2, owners, 128), I32),
            dma((heads,)),
            dma(()),
        ],
        compiler_params=limit(24),
        name="plan_and_pack",
    )(me, from_all, count, start, pltpu.with_memory_space_constraint(in_order, pltpu.HBM))

    def pack(capacity):
        return pl.pallas_call(
            functools.partial(pack_kernel, capacity, rounds),
            out_shape=jax.ShapeDtypeStruct((owners, FIELDS * capacity, HEAD), BF16),
            in_specs=[smem(), whole()],
            out_specs=whole(),
            scratch_shapes=[all_rows, pltpu.VMEM((FIELDS, pad_rows(capacity), HEAD), F32)],
            compiler_params=limit(24),
            name="pack",
        )(pack_table, in_order)

    def exchange(capacity, sending):
        owned = lax.all_to_all(sending, "seq", 0, 0, tiled=True)
        results = pl.pallas_call(
            functools.partial(attend_kernel, capacity, rounds),
            out_shape=jax.ShapeDtypeStruct(owned.shape, BF16),
            in_specs=[smem(), whole()],
            out_specs=whole(),
            scratch_shapes=[
                pltpu.VMEM((owners * FIELDS, pad_rows(capacity), HEAD), F32),
                pltpu.VMEM((owners * FIELDS, pad_rows(capacity), HEAD), F32),
                pltpu.VMEM((FIELDS, most + BLOCK + SLOT, HEAD), F32),
                pltpu.VMEM((FIELDS - 1, most, HEAD), BF16),
                pltpu.VMEM((FIELDS, most + SLOT, HEAD), F32),
            ],
            compiler_params=limit(36 if capacity <= TIGHT else 44),
            name="attend",
        )(mine_table, owned)
        returned = lax.all_to_all(results, "seq", 0, 0, tiled=True)
        return pl.pallas_call(
            functools.partial(unpack_kernel, capacity),
            out_shape=(jax.ShapeDtypeStruct(queries.shape, BF16),) * 4,
            in_specs=[smem(), smem(), whole(), whole()],
            out_specs=(in_hbm(),) * 4,
            scratch_shapes=[
                pltpu.VMEM((FIELDS, owners * padded, HEAD), F32),
                pltpu.VMEM((FIELDS, tokens + SLOT, HEAD), F32),
                all_fields,
                dma((heads, FIELDS, blocks)),
            ],
            compiler_params=limit(28),
            name="unpack",
        )(back_table, start, place, returned)

    def again(state):
        return (jnp.zeros((1,), I32), *exchange(rounds * SLOT, pack(rounds * SLOT)))

    tight = exchange(TIGHT, sending)
    return lax.while_loop(lambda state: state[0][0] > TIGHT, again, (heaviest, *tight))[1:]


def solution(mesh):
    spec = P("seq", "head")
    return jax.shard_map(
        on_device, mesh=mesh, in_specs=(spec,) * 5, out_specs=(spec,) * 4, check_vma=False
    )
```

```python
import functools

import jax
import jax.numpy as jnp
from jax import lax
from jax.experimental import pallas as pl
from jax.experimental.pallas import tpu as pltpu
from jax.sharding import PartitionSpec as P

HEAD = 128
CLUSTERS = 64
SLOT = 24
BLOCK = 256
FIELDS = 4
TIGHT = 144
DEALS = (
    (0, 0, 0, 0, 0, 0),
    (27, 20, 16, 8, 9, 1),
    (2, 0, 5, 26, 20, 29),
    (11, 30, 23, 3, 17, 6),
    (18, 7, 12, 31, 2, 14),
    (5, 25, 28, 10, 19, 22),
    (21, 13, 1, 15, 24, 4),
    (9, 3, 30, 6, 11, 27),
)
LOG2_E = 1.4426950408889634
F32 = jnp.float32
BF16 = jnp.bfloat16
I32 = jnp.int32


def iota(shape, dim):
    return lax.broadcasted_iota(I32, shape, dim)


def against(a, b):
    return lax.dot_general(a, b, (((1,), (1,)), ((), ())), preferred_element_type=F32)


def across(a, b):
    return lax.dot_general(a, b, (((0,), (0,)), ((), ())), preferred_element_type=F32)


def limit(mib):
    return pltpu.CompilerParams(vmem_limit_bytes=mib * 1024 * 1024)


def smem():
    return pl.BlockSpec(memory_space=pltpu.SMEM)


def whole():
    return pl.BlockSpec(memory_space=pltpu.VMEM)


def in_hbm():
    return pl.BlockSpec(memory_space=pltpu.HBM)


def pad_rows(capacity):
    return (capacity + SLOT + 7) // 8 * 8


def work_of(flops, moved):
    return pl.CostEstimate(flops=flops, bytes_accessed=moved, transcendentals=0)


def marks_of(ids_ref):
    heads, tokens = ids_ref.shape
    return jnp.concatenate(
        [
            (ids_ref[h : h + 1, :] == iota((CLUSTERS, tokens), 0)).astype(BF16)
            for h in range(heads)
        ],
        axis=0,
    )


def count_kernel(ids_ref, count_ref):
    count_line = against(jnp.ones((8, ids_ref.shape[1]), BF16), marks_of(ids_ref))
    for k in range(count_line.shape[1] // 128):
        part = count_line[None, :1, k * 128 : (k + 1) * 128].astype(I32)
        count_ref[:, k : k + 1, :] = jnp.broadcast_to(part, (count_ref.shape[0], 1, 128))


def sort_kernel(ids_ref, q_ref, k_ref, v_ref, g_ref, out_ref, place_ref, own_ref, start_ref, *scratch):
    taken, given, in_sems, out_sems = scratch
    heads, tokens = ids_ref.shape
    pairs = heads * CLUSTERS
    arriving = []
    for h in range(heads):
        copies = [
            pltpu.make_async_copy(
                ref.at[:, pl.ds(h * HEAD, HEAD)], taken.at[h, a], in_sems.at[h, a]
            )
            for a, ref in enumerate((q_ref, k_ref, v_ref, g_ref))
        ]
        for copy in copies:
            copy.start()
        arriving.append(copies)

    marks = marks_of(ids_ref)
    row, col = iota((pairs, pairs), 0), iota((pairs, pairs), 1)
    earlier = ((col < row) & (col // CLUSTERS == row // CLUSTERS)).astype(BF16)
    count_wide = against(marks, jnp.ones((128, tokens), BF16))
    start_wide = jnp.dot(earlier, count_wide.astype(BF16), preferred_element_type=F32)
    count_line = against(jnp.ones((8, tokens), BF16), marks)
    own_ref[...] = count_line.astype(I32)
    start_ref[...] = against(count_line.astype(BF16), earlier).astype(I32)
    upper = (iota((BLOCK, BLOCK), 0) < iota((BLOCK, BLOCK), 1)).astype(BF16)
    carry = start_wide[:, :1]
    for b in range(tokens // BLOCK):
        part = marks[:, b * BLOCK : (b + 1) * BLOCK]
        before = jnp.dot(part, upper, preferred_element_type=F32) + carry
        wide = part.astype(F32)
        carry = carry + jnp.sum(wide, axis=1, keepdims=True)
        place = wide * before
        for h in range(heads):
            place_ref[h : h + 1, b * BLOCK : (b + 1) * BLOCK] = jnp.sum(
                place[h * CLUSTERS : (h + 1) * CLUSTERS], axis=0, keepdims=True
            ).astype(I32)

    leaving = []
    for h in range(heads):
        for copy in arriving[h]:
            copy.wait()
        fields = jnp.concatenate([taken[h, a] for a in range(FIELDS)], axis=1)
        for b in range(tokens // BLOCK):
            part = slice(b * BLOCK, (b + 1) * BLOCK)
            select = (place_ref[h : h + 1, :] == iota((BLOCK, tokens), 0) + b * BLOCK).astype(BF16)
            rows = jnp.dot(select, fields, preferred_element_type=F32).astype(BF16)
            for a in range(FIELDS):
                given[h, a, part, :] = rows[:, a * HEAD : (a + 1) * HEAD]
            part = pl.ds(b * BLOCK, BLOCK)
            copy = pltpu.make_async_copy(
                given.at[h, :, part], out_ref.at[h, :, part], out_sems.at[h, b]
            )
            copy.start()
            leaving.append(copy)
    for copy in leaving:
        copy.wait()


def plan(padded, tokens, me_ref, from_ref, own_ref, start_ref, pack_ref, mine_ref, back_ref, most_ref):
    owners, pairs = from_ref.shape[0], own_ref.shape[1]
    rounds = pairs // owners
    deals = len(DEALS)
    counts = jnp.concatenate(
        [from_ref[:, k : k + 1, :].reshape(owners, 128) for k in range(pairs // 128)], axis=1
    )
    counts = counts.astype(F32)
    row, col = iota((pairs, pairs), 0), iota((pairs, pairs), 1)
    total_line = jnp.sum(counts, axis=0, keepdims=True)
    total_col = jnp.sum(jnp.where(row == col, total_line, 0.0), axis=1, keepdims=True)
    ahead = (total_line > total_col) | ((total_line == total_col) & (col < row))
    rank_col = jnp.sum(ahead.astype(F32), axis=1, keepdims=True)
    at_rank = rank_col == col.astype(F32)
    both_col = total_col * float(pairs) + iota((pairs, 1), 0).astype(F32)
    both_line = jnp.sum(jnp.where(at_rank, both_col, 0.0), axis=0, keepdims=True)
    seats = deals * owners
    seat = iota((seats, 1), 0)
    device, deal = seat % owners, seat // owners
    lane = iota((seats, pairs), 1).astype(F32)
    near, far = iota((seats, seats), 0), iota((seats, seats), 1)
    together = near // owners == far // owners
    load = jnp.zeros((seats, 1), F32)
    lists = jnp.zeros((seats, 128), F32)
    owned = jnp.zeros((seats, pairs), F32)
    for r in range(rounds):
        if r >= len(DEALS[0]):
            load_line = jnp.sum(jnp.where(near == far, load, 0.0), axis=0, keepdims=True)
            lighter = (load_line < load) | ((load_line == load) & (far < near))
            turn = jnp.sum((lighter & together).astype(F32), axis=1, keepdims=True)
        else:
            shift = jnp.zeros((seats, 1), I32)
            for c in range(deals):
                shift = jnp.where(deal == c, DEALS[c][r], shift)
            turn = (device + shift) % owners
            if r % 2 == 1:
                turn = owners - 1 - turn
            turn = turn.astype(F32)
        pick = lane == turn + float(r * owners)
        both = jnp.sum(jnp.where(pick, both_line, 0.0), axis=1, keepdims=True)
        size = jnp.floor(both * (1.0 / pairs))
        item = both - size * float(pairs)
        load = load + size
        lists = jnp.where(iota((seats, 128), 1) == r, item, lists)
        owned = jnp.where(lane == item, 1.0, owned)
    sent = against(counts.astype(BF16), owned.astype(BF16))
    heaviest = jnp.max(sent, axis=0, keepdims=True)
    seat_line = iota((1, seats), 1)
    least = None
    for c in range(deals):
        most = jnp.max(
            jnp.where(seat_line // owners == c, heaviest, 0.0), axis=1, keepdims=True
        )
        mine = lists[c * owners : (c + 1) * owners]
        if least is None:
            least, chosen = most, mine
        else:
            chosen = jnp.where(most < least, mine, chosen)
            least = jnp.minimum(least, most)
    most_ref[0] = jnp.max(least).astype(I32)

    lane = iota((owners, pairs), 1)
    own_line = own_ref[:1, :].astype(F32)
    begin_line = (start_ref[:1, :] + iota((1, pairs), 1) // CLUSTERS * tokens).astype(F32)
    place = jnp.zeros((owners, 1), F32)
    sources, places = jnp.zeros((owners, 128), F32), jnp.zeros((owners, 128), F32)
    back = jnp.zeros((1, pairs), F32)
    home = iota((owners, 1), 0).astype(F32) * float(padded)
    slot = iota((owners, 128), 1)
    for r in range(rounds):
        pick = lane.astype(F32) == chosen[:, r : r + 1]
        sources = jnp.where(
            slot == r, jnp.sum(jnp.where(pick, begin_line, 0.0), axis=1, keepdims=True), sources
        )
        places = jnp.where(slot == r, place, places)
        back = back + jnp.sum(jnp.where(pick, home + place, 0.0), axis=0, keepdims=True)
        place = place + jnp.sum(jnp.where(pick, own_line, 0.0), axis=1, keepdims=True)
    pack_ref[0] = sources.astype(I32)
    pack_ref[1] = places.astype(I32)
    back_ref[...] = jnp.broadcast_to(back, back_ref.shape).astype(I32)

    items = jnp.sum(jnp.where(iota((owners, 128), 0) == me_ref[0], chosen, 0.0), axis=0, keepdims=True)
    square = iota((128, 128), 0), iota((128, 128), 1)
    item_col = jnp.sum(jnp.where(square[0] == square[1], items, 0.0), axis=1, keepdims=True)
    held = (iota((128, pairs), 1).astype(F32) == item_col) & (iota((128, pairs), 0) < rounds)
    mine = against(counts.astype(BF16), held.astype(BF16)).astype(BF16)
    earlier = (square[0] < square[1]).astype(BF16)
    mine_ref[0] = jnp.dot(mine, earlier, preferred_element_type=F32).astype(I32)
    lower = (iota((owners + 8, owners), 1) < iota((owners + 8, owners), 0)).astype(BF16)
    filled = jnp.dot(lower, mine, preferred_element_type=F32).astype(I32)
    mine_ref[1] = filled[:owners]
    mine_ref[2] = jnp.broadcast_to(filled[owners : owners + 1], (owners, 128))


def fill(capacity, rounds, table, rows, block, out_ref):
    def one_owner(d, _):
        for j in range(rounds):
            source = table[0, d, j]
            target = jnp.minimum(table[1, d, j], capacity)
            for a in range(FIELDS):
                block[a, pl.ds(target, SLOT), :] = rows[a, pl.ds(source, SLOT), :]
        for a in range(FIELDS):
            out_ref[d, a * capacity : (a + 1) * capacity, :] = block[a, :capacity, :].astype(BF16)
        return 0

    lax.fori_loop(0, out_ref.shape[0], one_owner, 0, unroll=4)


def widen_heads(sorted_ref, rows):
    heads, _, tokens, _ = sorted_ref.shape
    for h in range(heads):
        for a in range(FIELDS):
            rows[a, h * tokens : (h + 1) * tokens, :] = sorted_ref[h, a].astype(F32)


def pack_kernel(capacity, rounds, table_ref, sorted_ref, out_ref, rows, block):
    widen_heads(sorted_ref, rows)
    fill(capacity, rounds, table_ref, rows, block, out_ref)


def plan_and_pack_kernel(capacity, rounds, padded, me_ref, from_ref, own_ref, start_ref, sorted_ref, *refs):
    out_ref, pack_ref, mine_ref, back_ref, most_ref, taken, rows, block, table, in_sems, table_sem = refs
    heads, _, tokens, _ = sorted_ref.shape
    arriving = [
        pltpu.make_async_copy(sorted_ref.at[h], taken.at[h], in_sems.at[h]) for h in range(heads)
    ]
    for copy in arriving:
        copy.start()
    plan(padded, tokens, me_ref, from_ref, own_ref, start_ref, pack_ref, mine_ref, back_ref, most_ref)
    copy = pltpu.make_async_copy(pack_ref, table, table_sem)
    copy.start()
    for h in range(heads):
        arriving[h].wait()
        for a in range(FIELDS):
            rows[a, h * tokens : (h + 1) * tokens, :] = taken[h, a].astype(F32)
    copy.wait()
    fill(capacity, rounds, table, rows, block, out_ref)


def attend_kernel(capacity, rounds, table_ref, in_ref, out_ref, *scratch):
    arrived, leaving, gathered, work, done = scratch
    sources = in_ref.shape[0]
    most = work.shape[1]
    factor = float(HEAD) ** -0.5

    def widen(s, _):
        for a in range(FIELDS):
            arrived[s * FIELDS + a, :capacity, :] = in_ref[
                s, a * capacity : (a + 1) * capacity, :
            ].astype(F32)
        return 0

    lax.fori_loop(0, sources, widen, 0, unroll=8)

    def cluster(n):
        size = n * BLOCK
        query, keys, values = (work[a, :size, :] for a in range(FIELDS - 1))
        scale = factor * LOG2_E
        below = iota((BLOCK, BLOCK), 0) <= iota((BLOCK, BLOCK), 1)
        keys_t = gathered[1, :size, :].T.astype(BF16)
        values_t = gathered[2, :size, :].T.astype(BF16)
        up_t = gathered[3, :size, :].T
        upstream_t = up_t.astype(BF16)
        cols = [slice(b * BLOCK, (b + 1) * BLOCK) for b in range(n)]
        upto = [slice(0, (b + 1) * BLOCK) for b in range(n)]
        scores = [against(keys[upto[b]], query[cols[b]]) for b in range(n)]
        weights, inverse = [], []
        for b in range(n):
            s = scores[b]
            last = jnp.where(below, s[b * BLOCK :], -jnp.inf)
            s = last if b == 0 else jnp.concatenate([s[: b * BLOCK], last], axis=0)
            weights.append(jnp.exp2((s - jnp.max(s, axis=0, keepdims=True)) * scale))
            inverse.append(1.0 / jnp.sum(weights[b], axis=0, keepdims=True))
        coarse = [(weights[b] * inverse[b]).astype(BF16) for b in range(n)]
        attended = [
            jnp.dot(values_t[:, upto[b]], coarse[b], preferred_element_type=F32)
            for b in range(n)
        ]
        for b in range(n):
            done[0, cols[b], :] = attended[b].T
        through = [
            jnp.dot(values[upto[b]], upstream_t[:, cols[b]], preferred_element_type=F32)
            for b in range(n)
        ]
        for k in range(n):
            part = jnp.concatenate([coarse[b][cols[k]] for b in range(k, n)], axis=1)
            done[3, cols[k], :] = against(part, upstream_t[:, k * BLOCK :])
        slope = []
        for b in range(n):
            row_dot = jnp.sum(
                up_t[:, cols[b]] * attended[b].astype(BF16).astype(F32), axis=0, keepdims=True
            )
            slope.append((weights[b] * ((through[b] - row_dot) * inverse[b])).astype(BF16))
        for b in range(n):
            done[1, cols[b], :] = (
                factor * jnp.dot(keys_t[:, upto[b]], slope[b], preferred_element_type=F32).T
            )
        for k in range(n):
            part = jnp.concatenate([slope[b][cols[k]] for b in range(k, n)], axis=1)
            done[2, cols[k], :] = factor * jnp.dot(
                part, query[k * BLOCK :], preferred_element_type=F32
            )

    def one(j, _):
        for s in range(sources):
            place, filled = jnp.minimum(table_ref[0, s, j], capacity), table_ref[1, s, j]
            for a in range(FIELDS):
                gathered[a, pl.ds(filled, SLOT), :] = arrived[
                    s * FIELDS + a, pl.ds(place, SLOT), :
                ]
        total = table_ref[2, 0, j]
        for a in range(FIELDS):
            gathered[a, pl.ds(total, BLOCK), :] = jnp.zeros((BLOCK, HEAD), F32)
        blocks = most // BLOCK
        for n in range(1, blocks + 1):
            enough = total > (n - 1) * BLOCK
            if n < blocks:
                enough = enough & (total <= n * BLOCK)

            @pl.when(enough)
            def _():
                for a in range(FIELDS - 1):
                    work[a, : n * BLOCK, :] = gathered[a, : n * BLOCK, :].astype(BF16)
                cluster(n)

        for s in range(sources):
            place, filled = jnp.minimum(table_ref[0, s, j], capacity), table_ref[1, s, j]
            for a in range(FIELDS):
                leaving[s * FIELDS + a, pl.ds(place, SLOT), :] = done[a, pl.ds(filled, SLOT), :]
        return 0

    lax.fori_loop(0, rounds, one, 0)

    def narrow(s, _):
        for a in range(FIELDS):
            out_ref[s, a * capacity : (a + 1) * capacity, :] = leaving[
                s * FIELDS + a, :capacity, :
            ].astype(BF16)
        return 0

    lax.fori_loop(0, sources, narrow, 0, unroll=8)


def unpack_kernel(capacity, back_ref, start_ref, place_ref, in_ref, *refs):
    out_refs, (wide, rows, given, out_sems) = refs[:FIELDS], refs[FIELDS:]
    owners, heads, tokens = in_ref.shape[0], given.shape[0], given.shape[2]
    padded = wide.shape[1] // owners

    def widen(d, _):
        place = pl.multiple_of(d * padded, 8)
        for a in range(FIELDS):
            wide[a, pl.ds(place, capacity), :] = in_ref[
                d, a * capacity : (a + 1) * capacity, :
            ].astype(F32)
        return 0

    lax.fori_loop(0, owners, widen, 0, unroll=8)
    lines = jnp.concatenate(
        [place_ref[...].astype(F32), jnp.zeros((128 - heads, tokens), F32)], axis=0
    )
    columns = lines.T.astype(I32)
    leaving = []
    for h in range(heads):
        for c in range(CLUSTERS):
            target = start_ref[0, h * CLUSTERS + c]
            source = back_ref[0, h * CLUSTERS + c]
            for a in range(FIELDS):
                rows[a, pl.ds(target, SLOT), :] = wide[a, pl.ds(source, SLOT), :]
        fields = jnp.concatenate([rows[a, :tokens, :].astype(BF16) for a in range(FIELDS)], axis=1)
        for b in range(tokens // BLOCK):
            part = slice(b * BLOCK, (b + 1) * BLOCK)
            select = (columns[part, h : h + 1] == iota((BLOCK, tokens), 1)).astype(BF16)
            result = jnp.dot(select, fields, preferred_element_type=F32).astype(BF16)
            for a in range(FIELDS):
                given[h, a, part, :] = result[:, a * HEAD : (a + 1) * HEAD]
            for a, ref in enumerate(out_refs):
                copy = pltpu.make_async_copy(
                    given.at[h, a, pl.ds(b * BLOCK, BLOCK)],
                    ref.at[pl.ds(b * BLOCK, BLOCK), pl.ds(h * HEAD, HEAD)],
                    out_sems.at[h, a, b],
                )
                copy.start()
                leaving.append(copy)
    for copy in leaving:
        copy.wait()


def on_device(queries, key_rows, value_rows, grad_out, cluster_ids):
    tokens, heads = cluster_ids.shape
    owners = lax.axis_size("seq")
    pairs = heads * CLUSTERS
    rounds = pairs // owners
    most = owners * SLOT
    me = lax.axis_index("seq").astype(I32).reshape(1)

    ids = cluster_ids.T
    padded = pad_rows(rounds * SLOT)
    blocks = tokens // BLOCK
    dma = pltpu.SemaphoreType.DMA
    all_fields = pltpu.VMEM((heads, FIELDS, tokens, HEAD), BF16)
    all_rows = pltpu.VMEM((FIELDS, heads * tokens + SLOT, HEAD), F32)

    to_all = pl.pallas_call(
        count_kernel,
        out_shape=jax.ShapeDtypeStruct((owners, 8, 128), I32),
        in_specs=[whole()],
        out_specs=whole(),
        compiler_params=limit(16),
        name="count",
    )(ids)
    from_all = lax.all_to_all(to_all, "seq", 0, 0, tiled=True)

    in_order, place, count, start = pl.pallas_call(
        sort_kernel,
        out_shape=(
            jax.ShapeDtypeStruct((heads, FIELDS, tokens, HEAD), BF16),
            jax.ShapeDtypeStruct((heads, tokens), I32),
            jax.ShapeDtypeStruct((8, pairs), I32),
            jax.ShapeDtypeStruct((8, pairs), I32),
        ),
        in_specs=[whole()] + [in_hbm()] * 4,
        out_specs=(in_hbm(),) + (whole(),) * 3,
        scratch_shapes=[
            all_fields,
            all_fields,
            dma((heads, FIELDS)),
            dma((heads, blocks)),
        ],
        cost_estimate=work_of(
            2 * heads * tokens * tokens * FIELDS * HEAD, 4 * FIELDS * heads * tokens * HEAD
        ),
        compiler_params=limit(24),
        name="sort",
    )(
        ids,
        *(
            pltpu.with_memory_space_constraint(field, pltpu.HBM)
            for field in (queries, key_rows, value_rows, grad_out)
        ),
    )

    sending, pack_table, mine_table, back_table, heaviest = pl.pallas_call(
        functools.partial(plan_and_pack_kernel, TIGHT, rounds, padded),
        out_shape=(
            jax.ShapeDtypeStruct((owners, FIELDS * TIGHT, HEAD), BF16),
            jax.ShapeDtypeStruct((2, owners, 128), I32),
            jax.ShapeDtypeStruct((3, owners, 128), I32),
            jax.ShapeDtypeStruct((8, pairs), I32),
            jax.ShapeDtypeStruct((1,), I32),
        ),
        in_specs=[smem()] + [whole()] * 3 + [in_hbm()],
        out_specs=(whole(),) * 4 + (smem(),),
        scratch_shapes=[
            all_fields,
            all_rows,
            pltpu.VMEM((FIELDS, pad_rows(TIGHT), HEAD), F32),
            pltpu.SMEM((2, owners, 128), I32),
            dma((heads,)),
            dma(()),
        ],
        compiler_params=limit(24),
        name="plan_and_pack",
    )(me, from_all, count, start, pltpu.with_memory_space_constraint(in_order, pltpu.HBM))

    def pack(capacity):
        return pl.pallas_call(
            functools.partial(pack_kernel, capacity, rounds),
            out_shape=jax.ShapeDtypeStruct((owners, FIELDS * capacity, HEAD), BF16),
            in_specs=[smem(), whole()],
            out_specs=whole(),
            scratch_shapes=[all_rows, pltpu.VMEM((FIELDS, pad_rows(capacity), HEAD), F32)],
            compiler_params=limit(24),
            name="pack",
        )(pack_table, in_order)

    def exchange(capacity, sending):
        owned = lax.all_to_all(sending, "seq", 0, 0, tiled=True)
        results = pl.pallas_call(
            functools.partial(attend_kernel, capacity, rounds),
            out_shape=jax.ShapeDtypeStruct(owned.shape, BF16),
            in_specs=[smem(), whole()],
            out_specs=whole(),
            scratch_shapes=[
                pltpu.VMEM((owners * FIELDS, pad_rows(capacity), HEAD), F32),
                pltpu.VMEM((owners * FIELDS, pad_rows(capacity), HEAD), F32),
                pltpu.VMEM((FIELDS, most + BLOCK + SLOT, HEAD), F32),
                pltpu.VMEM((FIELDS - 1, most, HEAD), BF16),
                pltpu.VMEM((FIELDS, most + SLOT, HEAD), F32),
            ],
            compiler_params=limit(36 if capacity <= TIGHT else 44),
            name="attend",
        )(mine_table, owned)
        returned = lax.all_to_all(results, "seq", 0, 0, tiled=True)
        return pl.pallas_call(
            functools.partial(unpack_kernel, capacity),
            out_shape=(jax.ShapeDtypeStruct(queries.shape, BF16),) * 4,
            in_specs=[smem(), smem(), whole(), whole()],
            out_specs=(in_hbm(),) * 4,
            scratch_shapes=[
                pltpu.VMEM((FIELDS, owners * padded, HEAD), F32),
                pltpu.VMEM((FIELDS, tokens + SLOT, HEAD), F32),
                all_fields,
                dma((heads, FIELDS, blocks)),
            ],
            compiler_params=limit(28),
            name="unpack",
        )(back_table, start, place, returned)

    def again(state):
        return (jnp.zeros((1,), I32), *exchange(rounds * SLOT, pack(rounds * SLOT)))

    tight = exchange(TIGHT, sending)
    return lax.while_loop(lambda state: state[0][0] > TIGHT, again, (heaviest, *tight))[1:]


def solution(mesh):
    spec = P("seq", "head")
    return jax.shard_map(
        on_device, mesh=mesh, in_specs=(spec,) * 5, out_specs=(spec,) * 4, check_vma=False
    )
```

```python
import functools

import jax
import jax.numpy as jnp
from jax import lax
from jax.experimental import pallas as pl
from jax.experimental.pallas import tpu as pltpu
from jax.sharding import PartitionSpec as P

HEAD = 128
CLUSTERS = 64
SLOT = 24
BLOCK = 256
FIELDS = 4
TIGHT = 144
DEALS = (
    (0, 0, 0, 0, 0, 0),
    (27, 20, 16, 8, 9, 1),
    (2, 0, 5, 26, 20, 29),
    (11, 30, 23, 3, 17, 6),
    (18, 7, 12, 31, 2, 14),
    (5, 25, 28, 10, 19, 22),
    (21, 13, 1, 15, 24, 4),
    (9, 3, 30, 6, 11, 27),
)
LOG2_E = 1.4426950408889634
F32 = jnp.float32
BF16 = jnp.bfloat16
I32 = jnp.int32


def iota(shape, dim):
    return lax.broadcasted_iota(I32, shape, dim)


def against(a, b):
    return lax.dot_general(a, b, (((1,), (1,)), ((), ())), preferred_element_type=F32)


def across(a, b):
    return lax.dot_general(a, b, (((0,), (0,)), ((), ())), preferred_element_type=F32)


def limit(mib):
    return pltpu.CompilerParams(vmem_limit_bytes=mib * 1024 * 1024)


def smem():
    return pl.BlockSpec(memory_space=pltpu.SMEM)


def whole():
    return pl.BlockSpec(memory_space=pltpu.VMEM)


def in_hbm():
    return pl.BlockSpec(memory_space=pltpu.HBM)


def pad_rows(capacity):
    return (capacity + SLOT + 7) // 8 * 8


def work_of(flops, moved):
    return pl.CostEstimate(flops=flops, bytes_accessed=moved, transcendentals=0)


def marks_of(ids_ref):
    heads, tokens = ids_ref.shape
    return jnp.concatenate(
        [
            (ids_ref[h : h + 1, :] == iota((CLUSTERS, tokens), 0)).astype(BF16)
            for h in range(heads)
        ],
        axis=0,
    )


def count_kernel(ids_ref, count_ref):
    count_line = against(jnp.ones((8, ids_ref.shape[1]), BF16), marks_of(ids_ref))
    for k in range(count_line.shape[1] // 128):
        part = count_line[None, :1, k * 128 : (k + 1) * 128].astype(I32)
        count_ref[:, k : k + 1, :] = jnp.broadcast_to(part, (count_ref.shape[0], 1, 128))


def sort_kernel(ids_ref, q_ref, k_ref, v_ref, g_ref, out_ref, place_ref, own_ref, start_ref, *scratch):
    taken, given, in_sems, out_sems = scratch
    heads, tokens = ids_ref.shape
    pairs = heads * CLUSTERS
    arriving = []
    for h in range(heads):
        copies = [
            pltpu.make_async_copy(
                ref.at[:, pl.ds(h * HEAD, HEAD)], taken.at[h, a], in_sems.at[h, a]
            )
            for a, ref in enumerate((q_ref, k_ref, v_ref, g_ref))
        ]
        for copy in copies:
            copy.start()
        arriving.append(copies)

    marks = marks_of(ids_ref)
    row, col = iota((pairs, pairs), 0), iota((pairs, pairs), 1)
    earlier = ((col < row) & (col // CLUSTERS == row // CLUSTERS)).astype(BF16)
    count_wide = against(marks, jnp.ones((128, tokens), BF16))
    start_wide = jnp.dot(earlier, count_wide.astype(BF16), preferred_element_type=F32)
    count_line = against(jnp.ones((8, tokens), BF16), marks)
    own_ref[...] = count_line.astype(I32)
    start_ref[...] = against(count_line.astype(BF16), earlier).astype(I32)
    upper = (iota((BLOCK, BLOCK), 0) < iota((BLOCK, BLOCK), 1)).astype(BF16)
    carry = start_wide[:, :1]
    for b in range(tokens // BLOCK):
        part = marks[:, b * BLOCK : (b + 1) * BLOCK]
        before = jnp.dot(part, upper, preferred_element_type=F32) + carry
        wide = part.astype(F32)
        carry = carry + jnp.sum(wide, axis=1, keepdims=True)
        place = wide * before
        for h in range(heads):
            place_ref[h : h + 1, b * BLOCK : (b + 1) * BLOCK] = jnp.sum(
                place[h * CLUSTERS : (h + 1) * CLUSTERS], axis=0, keepdims=True
            ).astype(I32)

    leaving = []
    for h in range(heads):
        for copy in arriving[h]:
            copy.wait()
        fields = jnp.concatenate([taken[h, a] for a in range(FIELDS)], axis=1)
        for b in range(tokens // BLOCK):
            part = slice(b * BLOCK, (b + 1) * BLOCK)
            select = (place_ref[h : h + 1, :] == iota((BLOCK, tokens), 0) + b * BLOCK).astype(BF16)
            rows = jnp.dot(select, fields, preferred_element_type=F32).astype(BF16)
            for a in range(FIELDS):
                given[h, a, part, :] = rows[:, a * HEAD : (a + 1) * HEAD]
            part = pl.ds(b * BLOCK, BLOCK)
            copy = pltpu.make_async_copy(
                given.at[h, :, part], out_ref.at[h, :, part], out_sems.at[h, b]
            )
            copy.start()
            leaving.append(copy)
    for copy in leaving:
        copy.wait()


def plan(padded, tokens, me_ref, from_ref, own_ref, start_ref, pack_ref, mine_ref, back_ref, most_ref):
    owners, pairs = from_ref.shape[0], own_ref.shape[1]
    rounds = pairs // owners
    deals = len(DEALS)
    counts = jnp.concatenate(
        [from_ref[:, k : k + 1, :].reshape(owners, 128) for k in range(pairs // 128)], axis=1
    )
    counts = counts.astype(F32)
    row, col = iota((pairs, pairs), 0), iota((pairs, pairs), 1)
    total_line = jnp.sum(counts, axis=0, keepdims=True)
    total_col = jnp.sum(jnp.where(row == col, total_line, 0.0), axis=1, keepdims=True)
    ahead = (total_line > total_col) | ((total_line == total_col) & (col < row))
    rank_col = jnp.sum(ahead.astype(F32), axis=1, keepdims=True)
    at_rank = rank_col == col.astype(F32)
    both_col = total_col * float(pairs) + iota((pairs, 1), 0).astype(F32)
    both_line = jnp.sum(jnp.where(at_rank, both_col, 0.0), axis=0, keepdims=True)
    seats = deals * owners
    seat = iota((seats, 1), 0)
    device, deal = seat % owners, seat // owners
    lane = iota((seats, pairs), 1).astype(F32)
    near, far = iota((seats, seats), 0), iota((seats, seats), 1)
    together = near // owners == far // owners
    load = jnp.zeros((seats, 1), F32)
    lists = jnp.zeros((seats, 128), F32)
    owned = jnp.zeros((seats, pairs), F32)
    for r in range(rounds):
        if r >= len(DEALS[0]):
            load_line = jnp.sum(jnp.where(near == far, load, 0.0), axis=0, keepdims=True)
            lighter = (load_line < load) | ((load_line == load) & (far < near))
            turn = jnp.sum((lighter & together).astype(F32), axis=1, keepdims=True)
        else:
            shift = jnp.zeros((seats, 1), I32)
            for c in range(deals):
                shift = jnp.where(deal == c, DEALS[c][r], shift)
            turn = (device + shift) % owners
            if r % 2 == 1:
                turn = owners - 1 - turn
            turn = turn.astype(F32)
        pick = lane == turn + float(r * owners)
        both = jnp.sum(jnp.where(pick, both_line, 0.0), axis=1, keepdims=True)
        size = jnp.floor(both * (1.0 / pairs))
        item = both - size * float(pairs)
        load = load + size
        lists = jnp.where(iota((seats, 128), 1) == r, item, lists)
        owned = jnp.where(lane == item, 1.0, owned)
    sent = against(counts.astype(BF16), owned.astype(BF16))
    heaviest = jnp.max(sent, axis=0, keepdims=True)
    seat_line = iota((1, seats), 1)
    least = None
    for c in range(deals):
        most = jnp.max(
            jnp.where(seat_line // owners == c, heaviest, 0.0), axis=1, keepdims=True
        )
        mine = lists[c * owners : (c + 1) * owners]
        if least is None:
            least, chosen = most, mine
        else:
            chosen = jnp.where(most < least, mine, chosen)
            least = jnp.minimum(least, most)
    most_ref[0] = jnp.max(least).astype(I32)

    lane = iota((owners, pairs), 1)
    own_line = own_ref[:1, :].astype(F32)
    begin_line = (start_ref[:1, :] + iota((1, pairs), 1) // CLUSTERS * tokens).astype(F32)
    place = jnp.zeros((owners, 1), F32)
    moves = jnp.zeros((owners, 128), F32)
    back = jnp.zeros((1, pairs), F32)
    home = iota((owners, 1), 0).astype(F32) * float(padded)
    slot = iota((owners, 128), 1)
    for r in range(rounds):
        pick = lane.astype(F32) == chosen[:, r : r + 1]
        source = jnp.sum(jnp.where(pick, begin_line, 0.0), axis=1, keepdims=True)
        moves = jnp.where(slot == r, source, jnp.where(slot == rounds + r, place, moves))
        back = back + jnp.sum(jnp.where(pick, home + place, 0.0), axis=0, keepdims=True)
        place = place + jnp.sum(jnp.where(pick, own_line, 0.0), axis=1, keepdims=True)
    pack_ref[...] = moves.astype(I32)
    for k in range(pairs // 128):
        part = slice(k * 128, (k + 1) * 128)
        back_ref[k : k + 1, :] = back[:, part].astype(I32)
        back_ref[pairs // 128 + k : pairs // 128 + k + 1, :] = start_ref[:1, part]

    items = jnp.sum(jnp.where(iota((owners, 128), 0) == me_ref[0], chosen, 0.0), axis=0, keepdims=True)
    down, right = iota((128, 128), 0), iota((128, 128), 1)
    item_col = jnp.sum(jnp.where(right == down % rounds, items, 0.0), axis=1, keepdims=True)
    held = (iota((128, pairs), 1).astype(F32) == item_col) & (iota((128, pairs), 0) < 3 * rounds)
    mine = against(counts.astype(BF16), held.astype(BF16)).astype(BF16)
    begin = jnp.dot(mine, (down < right).astype(BF16), preferred_element_type=F32)
    lower = (iota((owners, owners), 1) < iota((owners, owners), 0)).astype(BF16)
    filled = jnp.dot(lower, mine, preferred_element_type=F32)
    total = jnp.dot(jnp.ones((owners, owners), BF16), mine, preferred_element_type=F32)
    mine_ref[...] = jnp.where(
        slot < rounds, begin, jnp.where(slot < 2 * rounds, filled, total)
    ).astype(I32)


def fill(capacity, rounds, table, rows, block, out_ref):
    def one_owner(d, _):
        for j in range(rounds):
            source = table[d, j]
            target = jnp.minimum(table[d, rounds + j], capacity)
            for a in range(FIELDS):
                block[a, pl.ds(target, SLOT), :] = rows[a, pl.ds(source, SLOT), :]
        for a in range(FIELDS):
            out_ref[d, a * capacity : (a + 1) * capacity, :] = block[a, :capacity, :].astype(BF16)
        return 0

    lax.fori_loop(0, out_ref.shape[0], one_owner, 0, unroll=4)


def widen_heads(sorted_ref, rows):
    heads, _, tokens, _ = sorted_ref.shape
    for h in range(heads):
        for a in range(FIELDS):
            rows[a, h * tokens : (h + 1) * tokens, :] = sorted_ref[h, a].astype(F32)


def pack_kernel(capacity, rounds, table_ref, sorted_ref, out_ref, rows, block):
    widen_heads(sorted_ref, rows)
    fill(capacity, rounds, table_ref, rows, block, out_ref)


def plan_and_pack_kernel(capacity, rounds, padded, me_ref, from_ref, own_ref, start_ref, sorted_ref, *refs):
    out_ref, pack_ref, mine_ref, back_ref, most_ref, taken, rows, block, table, in_sems, table_sem = refs
    heads, _, tokens, _ = sorted_ref.shape
    arriving = [
        pltpu.make_async_copy(sorted_ref.at[h], taken.at[h], in_sems.at[h]) for h in range(heads)
    ]
    for copy in arriving:
        copy.start()
    plan(padded, tokens, me_ref, from_ref, own_ref, start_ref, pack_ref, mine_ref, back_ref, most_ref)
    copy = pltpu.make_async_copy(pack_ref, table, table_sem)
    copy.start()
    for h in range(heads):
        arriving[h].wait()
        for a in range(FIELDS):
            rows[a, h * tokens : (h + 1) * tokens, :] = taken[h, a].astype(F32)
    copy.wait()
    fill(capacity, rounds, table, rows, block, out_ref)


def attend_kernel(capacity, rounds, table_ref, in_ref, out_ref, *scratch):
    arrived, leaving, gathered, work, done = scratch
    sources = in_ref.shape[0]
    most = work.shape[1]
    factor = float(HEAD) ** -0.5

    def widen(s, _):
        for a in range(FIELDS):
            arrived[s * FIELDS + a, :capacity, :] = in_ref[
                s, a * capacity : (a + 1) * capacity, :
            ].astype(F32)
        return 0

    lax.fori_loop(0, sources, widen, 0, unroll=8)

    def cluster(n):
        size = n * BLOCK
        query, keys, values = (work[a, :size, :] for a in range(FIELDS - 1))
        scale = factor * LOG2_E
        below = iota((BLOCK, BLOCK), 0) <= iota((BLOCK, BLOCK), 1)
        keys_t = gathered[1, :size, :].T.astype(BF16)
        values_t = gathered[2, :size, :].T.astype(BF16)
        up_t = gathered[3, :size, :].T
        upstream_t = up_t.astype(BF16)
        cols = [slice(b * BLOCK, (b + 1) * BLOCK) for b in range(n)]
        upto = [slice(0, (b + 1) * BLOCK) for b in range(n)]
        scores = [against(keys[upto[b]], query[cols[b]]) for b in range(n)]
        weights, inverse = [], []
        for b in range(n):
            s = scores[b]
            last = jnp.where(below, s[b * BLOCK :], -jnp.inf)
            s = last if b == 0 else jnp.concatenate([s[: b * BLOCK], last], axis=0)
            weights.append(jnp.exp2((s - jnp.max(s, axis=0, keepdims=True)) * scale))
            inverse.append(1.0 / jnp.sum(weights[b], axis=0, keepdims=True))
        coarse = [(weights[b] * inverse[b]).astype(BF16) for b in range(n)]
        attended = [
            jnp.dot(values_t[:, upto[b]], coarse[b], preferred_element_type=F32)
            for b in range(n)
        ]
        for b in range(n):
            done[0, cols[b], :] = attended[b].T
        through = [
            jnp.dot(values[upto[b]], upstream_t[:, cols[b]], preferred_element_type=F32)
            for b in range(n)
        ]
        for k in range(n):
            part = jnp.concatenate([coarse[b][cols[k]] for b in range(k, n)], axis=1)
            done[3, cols[k], :] = against(part, upstream_t[:, k * BLOCK :])
        slope = []
        for b in range(n):
            row_dot = jnp.sum(
                up_t[:, cols[b]] * attended[b].astype(BF16).astype(F32), axis=0, keepdims=True
            )
            slope.append((weights[b] * ((through[b] - row_dot) * inverse[b])).astype(BF16))
        for b in range(n):
            done[1, cols[b], :] = (
                factor * jnp.dot(keys_t[:, upto[b]], slope[b], preferred_element_type=F32).T
            )
        for k in range(n):
            part = jnp.concatenate([slope[b][cols[k]] for b in range(k, n)], axis=1)
            done[2, cols[k], :] = factor * jnp.dot(
                part, query[k * BLOCK :], preferred_element_type=F32
            )

    def one(j, _):
        for s in range(sources):
            place = jnp.minimum(table_ref[s, j], capacity)
            filled = table_ref[s, rounds + j]
            for a in range(FIELDS):
                gathered[a, pl.ds(filled, SLOT), :] = arrived[
                    s * FIELDS + a, pl.ds(place, SLOT), :
                ]
        total = table_ref[0, 2 * rounds + j]
        for a in range(FIELDS):
            gathered[a, pl.ds(total, BLOCK), :] = jnp.zeros((BLOCK, HEAD), F32)
        blocks = most // BLOCK
        for n in range(1, blocks + 1):
            enough = total > (n - 1) * BLOCK
            if n < blocks:
                enough = enough & (total <= n * BLOCK)

            @pl.when(enough)
            def _():
                for a in range(FIELDS - 1):
                    work[a, : n * BLOCK, :] = gathered[a, : n * BLOCK, :].astype(BF16)
                cluster(n)

        for s in range(sources):
            place = jnp.minimum(table_ref[s, j], capacity)
            filled = table_ref[s, rounds + j]
            for a in range(FIELDS):
                leaving[s * FIELDS + a, pl.ds(place, SLOT), :] = done[a, pl.ds(filled, SLOT), :]
        return 0

    lax.fori_loop(0, rounds, one, 0)

    def narrow(s, _):
        for a in range(FIELDS):
            out_ref[s, a * capacity : (a + 1) * capacity, :] = leaving[
                s * FIELDS + a, :capacity, :
            ].astype(BF16)
        return 0

    lax.fori_loop(0, sources, narrow, 0, unroll=8)


def unpack_kernel(capacity, table_ref, place_ref, in_ref, *refs):
    out_refs, (wide, rows, given, out_sems) = refs[:FIELDS], refs[FIELDS:]
    owners, heads, tokens = in_ref.shape[0], given.shape[0], given.shape[2]
    padded = wide.shape[1] // owners

    def widen(d, _):
        place = pl.multiple_of(d * padded, 8)
        for a in range(FIELDS):
            wide[a, pl.ds(place, capacity), :] = in_ref[
                d, a * capacity : (a + 1) * capacity, :
            ].astype(F32)
        return 0

    lax.fori_loop(0, owners, widen, 0, unroll=8)
    lines = jnp.concatenate(
        [place_ref[...].astype(F32), jnp.zeros((128 - heads, tokens), F32)], axis=0
    )
    columns = lines.T.astype(I32)
    leaving = []
    for h in range(heads):
        for c in range(CLUSTERS):
            row, lane = divmod(h * CLUSTERS + c, 128)
            source = table_ref[row, lane]
            target = table_ref[heads * CLUSTERS // 128 + row, lane]
            for a in range(FIELDS):
                rows[a, pl.ds(target, SLOT), :] = wide[a, pl.ds(source, SLOT), :]
        fields = jnp.concatenate([rows[a, :tokens, :].astype(BF16) for a in range(FIELDS)], axis=1)
        for b in range(tokens // BLOCK):
            part = slice(b * BLOCK, (b + 1) * BLOCK)
            select = (columns[part, h : h + 1] == iota((BLOCK, tokens), 1)).astype(BF16)
            result = jnp.dot(select, fields, preferred_element_type=F32).astype(BF16)
            for a in range(FIELDS):
                given[h, a, part, :] = result[:, a * HEAD : (a + 1) * HEAD]
            for a, ref in enumerate(out_refs):
                copy = pltpu.make_async_copy(
                    given.at[h, a, pl.ds(b * BLOCK, BLOCK)],
                    ref.at[pl.ds(b * BLOCK, BLOCK), pl.ds(h * HEAD, HEAD)],
                    out_sems.at[h, a, b],
                )
                copy.start()
                leaving.append(copy)
    for copy in leaving:
        copy.wait()


def on_device(queries, key_rows, value_rows, grad_out, cluster_ids):
    tokens, heads = cluster_ids.shape
    owners = lax.axis_size("seq")
    pairs = heads * CLUSTERS
    rounds = pairs // owners
    most = owners * SLOT
    me = lax.axis_index("seq").astype(I32).reshape(1)

    ids = cluster_ids.T
    padded = pad_rows(rounds * SLOT)
    blocks = tokens // BLOCK
    dma = pltpu.SemaphoreType.DMA
    all_fields = pltpu.VMEM((heads, FIELDS, tokens, HEAD), BF16)
    all_rows = pltpu.VMEM((FIELDS, heads * tokens + SLOT, HEAD), F32)

    to_all = pl.pallas_call(
        count_kernel,
        out_shape=jax.ShapeDtypeStruct((owners, 8, 128), I32),
        in_specs=[whole()],
        out_specs=whole(),
        compiler_params=limit(16),
        name="count",
    )(ids)
    from_all = lax.all_to_all(to_all, "seq", 0, 0, tiled=True)

    in_order, place, count, start = pl.pallas_call(
        sort_kernel,
        out_shape=(
            jax.ShapeDtypeStruct((heads, FIELDS, tokens, HEAD), BF16),
            jax.ShapeDtypeStruct((heads, tokens), I32),
            jax.ShapeDtypeStruct((8, pairs), I32),
            jax.ShapeDtypeStruct((8, pairs), I32),
        ),
        in_specs=[whole()] + [in_hbm()] * 4,
        out_specs=(in_hbm(),) + (whole(),) * 3,
        scratch_shapes=[
            all_fields,
            all_fields,
            dma((heads, FIELDS)),
            dma((heads, blocks)),
        ],
        cost_estimate=work_of(
            2 * heads * tokens * tokens * FIELDS * HEAD, 4 * FIELDS * heads * tokens * HEAD
        ),
        compiler_params=limit(24),
        name="sort",
    )(
        ids,
        *(
            pltpu.with_memory_space_constraint(field, pltpu.HBM)
            for field in (queries, key_rows, value_rows, grad_out)
        ),
    )

    sending, pack_table, mine_table, back_table, heaviest = pl.pallas_call(
        functools.partial(plan_and_pack_kernel, TIGHT, rounds, padded),
        out_shape=(
            jax.ShapeDtypeStruct((owners, FIELDS * TIGHT, HEAD), BF16),
            jax.ShapeDtypeStruct((owners, 128), I32),
            jax.ShapeDtypeStruct((owners, 128), I32),
            jax.ShapeDtypeStruct((2 * pairs // 128, 128), I32),
            jax.ShapeDtypeStruct((1,), I32),
        ),
        in_specs=[smem()] + [whole()] * 3 + [in_hbm()],
        out_specs=(whole(),) * 4 + (smem(),),
        scratch_shapes=[
            all_fields,
            all_rows,
            pltpu.VMEM((FIELDS, pad_rows(TIGHT), HEAD), F32),
            pltpu.SMEM((owners, 128), I32),
            dma((heads,)),
            dma(()),
        ],
        compiler_params=limit(24),
        name="plan_and_pack",
    )(me, from_all, count, start, pltpu.with_memory_space_constraint(in_order, pltpu.HBM))

    def pack(capacity):
        return pl.pallas_call(
            functools.partial(pack_kernel, capacity, rounds),
            out_shape=jax.ShapeDtypeStruct((owners, FIELDS * capacity, HEAD), BF16),
            in_specs=[smem(), whole()],
            out_specs=whole(),
            scratch_shapes=[all_rows, pltpu.VMEM((FIELDS, pad_rows(capacity), HEAD), F32)],
            compiler_params=limit(24),
            name="pack",
        )(pack_table, in_order)

    def exchange(capacity, sending):
        owned = lax.all_to_all(sending, "seq", 0, 0, tiled=True)
        results = pl.pallas_call(
            functools.partial(attend_kernel, capacity, rounds),
            out_shape=jax.ShapeDtypeStruct(owned.shape, BF16),
            in_specs=[smem(), whole()],
            out_specs=whole(),
            scratch_shapes=[
                pltpu.VMEM((owners * FIELDS, pad_rows(capacity), HEAD), F32),
                pltpu.VMEM((owners * FIELDS, pad_rows(capacity), HEAD), F32),
                pltpu.VMEM((FIELDS, most + BLOCK + SLOT, HEAD), F32),
                pltpu.VMEM((FIELDS - 1, most, HEAD), BF16),
                pltpu.VMEM((FIELDS, most + SLOT, HEAD), F32),
            ],
            compiler_params=limit(36 if capacity <= TIGHT else 44),
            name="attend",
        )(mine_table, owned)
        returned = lax.all_to_all(results, "seq", 0, 0, tiled=True)
        return pl.pallas_call(
            functools.partial(unpack_kernel, capacity),
            out_shape=(jax.ShapeDtypeStruct(queries.shape, BF16),) * 4,
            in_specs=[smem(), whole(), whole()],
            out_specs=(in_hbm(),) * 4,
            scratch_shapes=[
                pltpu.VMEM((FIELDS, owners * padded, HEAD), F32),
                pltpu.VMEM((FIELDS, tokens + SLOT, HEAD), F32),
                all_fields,
                dma((heads, FIELDS, blocks)),
            ],
            compiler_params=limit(28),
            name="unpack",
        )(back_table, place, returned)

    def again(state):
        return (jnp.zeros((1,), I32), *exchange(rounds * SLOT, pack(rounds * SLOT)))

    tight = exchange(TIGHT, sending)
    return lax.while_loop(lambda state: state[0][0] > TIGHT, again, (heaviest, *tight))[1:]


def solution(mesh):
    spec = P("seq", "head")
    return jax.shard_map(
        on_device, mesh=mesh, in_specs=(spec,) * 5, out_specs=(spec,) * 4, check_vma=False
    )
```
